256 devices in a mesh: dp: 32 (over z_lo, x, y), space: 8 (over z_hi, core).
Axes of the slice: x: 4, y: 4, z: 8 (z_hi: 4, z_lo: 2; z = z_hi * 2 + z_lo), core: 2. Of those that a mesh axis runs over, the one named last changes fastest.
Arguments:
- images: bfloat16 [32, 1024, 1024], P('dp', 'space'), may hold values from -6 to 6
- cotangent: bfloat16 [32, 1024, 1024], P('dp', 'space'), may hold values from -6 to 6
- w_qkv: bfloat16 [1024, 3072], P('dp'), may hold values from -0.1875 to 0.1875
- w_out: bfloat16 [1024, 1024], P('dp'), may hold values from -0.1875 to 0.1875
- film: bfloat16 [1000, 2048], replicated, may hold values from -1 to 1
- timesteps: int32 [32], P('dp'), may hold values from 0 to 999
Outputs:
- branch_grad: bfloat16 [32, 1024, 1024], P('dp', 'space')
- grad_qkv: float32 [1024, 3072], P('dp')
- grad_out: float32 [1024, 1024], P('dp')
The draws below stay inside these ranges and needn't reach their ends.
All inputs are finite; a program needn't handle non-finite values.
Results may differ from the reference program's by a relative error of at most 0.034.
Values may be sent and summed in bfloat16 or wider, within the bound.
No kernel may reach another device: no remote copies, remote signals or barrier semaphores. Data moves between devices by JAX's collectives and lax.ppermute only.
A program may use at most 128 MiB of HBM per device.

```python
import jax
import jax.numpy as jnp
from jax import lax

HEADS = 16
HEAD = 64
C = 1024
STEPS = 1000
CELLS = 1024
BATCH = 32


def draw_film(key, part):
    key = jax.random.fold_in(key, 7)
    key_a, key_b = jax.random.split(key, 2)
    scale_part = jnp.clip(0.3 * jax.random.normal(key_a, (STEPS, C), jnp.float32), -0.9, 0.9)
    shift_part = jnp.clip(0.5 * jax.random.normal(key_b, (STEPS, C), jnp.float32), -1.0, 1.0)
    return jnp.concatenate([scale_part, shift_part], 1).astype(jnp.bfloat16)


def plant(values, stream_key, smallest, high):
    longest = values.shape.index(max(values.shape))
    spots = []
    for shift in (0, 1):
        where = [jax.random.randint(jax.random.fold_in(stream_key, axis), (), 0, length) for axis, length in enumerate(values.shape)]
        where[longest] = (where[longest] + shift) % values.shape[longest]
        spots.append(tuple(where))
    return values.at[spots[0]].set(smallest).at[spots[1]].set(high)


def shard_levels(rng, shape, cuts, smallest, largest):
    level, own = 1.0, jax.random.fold_in(rng, 6)
    for axis_at, parts in cuts:
        steps = jnp.exp(jax.random.uniform(jax.random.fold_in(own, axis_at), (parts,), jnp.float32, smallest / len(cuts), largest / len(cuts)))
        level = level * jnp.repeat(steps, shape[axis_at] // parts).reshape([-1 if axis == axis_at else 1 for axis in range(len(shape))])
    return level


def scatter_about(stream_key, shape, width, most, cuts=(), held_as=jnp.bfloat16):
    entries = width * jax.random.normal(stream_key, shape, jnp.float32)
    if cuts:
        entries = entries * shard_levels(stream_key, shape, cuts, -0.22, 0.18)
    return jnp.clip(entries, -most, most).astype(held_as)


def setup_inputs(seed: int = 0) -> dict:
    key_of = jax.random.split(jax.random.key(seed), 7)
    return {
        "images": scatter_about(key_of[0], (BATCH, CELLS, C), 1.0, 6.0, ((0, 32), (1, 8))),
        "cotangent": scatter_about(key_of[1], (BATCH, CELLS, C), 1.0, 6.0, ((0, 32), (1, 8))),
        "w_qkv": scatter_about(key_of[2], (C, 3 * C), C ** -0.5, 0.1875, ((0, 32),)),
        "w_out": scatter_about(key_of[3], (C, C), C ** -0.5, 0.1875, ((0, 32),)),
        "film": draw_film(jax.random.fold_in(key_of[6], 71), 0),
        "timesteps": plant(jax.random.randint(key_of[5], (BATCH,), 0, STEPS), jax.random.fold_in(key_of[5], 1), 0, STEPS - 1).astype(jnp.int32),
    }


def one_image(w_qkv, w_out, carry, item):
    image, cot, feature_row = item
    channel_width = C
    xf = image.astype(jnp.float32)
    mean_x = lax.optimization_barrier(jnp.mean(xf, -1, keepdims=True))
    centered_input = xf - mean_x
    inverse_deviation = lax.rsqrt(lax.optimization_barrier(jnp.mean(centered_input * centered_input, -1, keepdims=True)) + 1e-05)
    normalized_input = centered_input * inverse_deviation
    scale_factor = 1.0 + feature_row[:channel_width]
    normalized_output = (normalized_input * scale_factor + feature_row[channel_width:]).astype(jnp.bfloat16)
    qkv = jnp.dot(normalized_output, w_qkv, preferred_element_type=jnp.float32).astype(jnp.bfloat16)
    query = qkv[:, :channel_width].reshape(CELLS, HEADS, HEAD).astype(jnp.float32)
    keys = qkv[:, channel_width:2 * channel_width].reshape(CELLS, HEADS, HEAD).astype(jnp.float32)
    values = qkv[:, 2 * channel_width:].reshape(CELLS, HEADS, HEAD).astype(jnp.float32)
    scores = jnp.einsum('qhd,khd->hqk', query, keys) * 0.125
    top = lax.optimization_barrier(jnp.max(scores, -1, keepdims=True))
    lse = top + jnp.log(lax.optimization_barrier(jnp.sum(jnp.exp(scores - top), -1, keepdims=True)))
    probs = jnp.exp(scores - lse)
    pb = probs.astype(jnp.bfloat16).astype(jnp.float32)
    attended = jnp.einsum('hqk,khd->qhd', pb, values).astype(jnp.bfloat16)
    d_att = jnp.dot(cot, w_out.T, preferred_element_type=jnp.float32).astype(jnp.bfloat16)
    att_flat = attended.reshape(CELLS, channel_width)
    grad_o = jnp.dot(att_flat.T, cot, preferred_element_type=jnp.float32)
    d_att3 = d_att.reshape(CELLS, HEADS, HEAD).astype(jnp.float32)
    delta = lax.optimization_barrier(jnp.sum(d_att3 * attended.astype(jnp.float32), -1))
    dprob = jnp.einsum('qhd,khd->hqk', d_att3, values)
    dscore = (probs * (dprob - delta.T[:, :, None])).astype(jnp.bfloat16).astype(jnp.float32)
    dquery = (0.125 * jnp.einsum('hqk,khd->qhd', dscore, keys)).astype(jnp.bfloat16)
    dkey = (0.125 * jnp.einsum('hqk,qhd->khd', dscore, query)).astype(jnp.bfloat16)
    dval = jnp.einsum('hqk,qhd->khd', pb, d_att3).astype(jnp.bfloat16)
    dqkv = jnp.concatenate([dquery.reshape(CELLS, channel_width), dkey.reshape(CELLS, channel_width), dval.reshape(CELLS, channel_width)], -1)
    grad_q = jnp.dot(normalized_output.T, dqkv, preferred_element_type=jnp.float32)
    dnormed = jnp.dot(dqkv, w_qkv.T, preferred_element_type=jnp.float32)
    normalized_gradient = dnormed * scale_factor
    residual_branch = inverse_deviation * (normalized_gradient - lax.optimization_barrier(jnp.mean(normalized_gradient, -1, keepdims=True)) - normalized_input * lax.optimization_barrier(jnp.mean(normalized_gradient * normalized_input, -1, keepdims=True)))
    return ((carry[0] + grad_q, carry[1] + grad_o), residual_branch.astype(jnp.bfloat16))

def reference(images, cotangent, w_qkv, w_out, film, timesteps):
    feature_rows = film[timesteps].astype(jnp.float32)
    init = (jnp.zeros((C, 3 * C), jnp.float32), jnp.zeros((C, C), jnp.float32))
    step = lambda carry, item: one_image(w_qkv, w_out, carry, item)
    sums, branch_grad = lax.scan(step, init, (images, cotangent, feature_rows))
    return (branch_grad, sums[0], sums[1])
```

```python
import jax
import jax.numpy as jnp
from jax import lax
from jax.experimental import pallas as pl
from jax.experimental.pallas import tpu as pltpu
from jax.sharding import PartitionSpec as P

C = 1024
Z = 4
PAIR = 128
BLOCK = 256
F32 = jnp.float32
BF16 = jnp.bfloat16


def nt(a, b):
    return lax.dot_general(a, b, (((1,), (1,)), ((), ())), preferred_element_type=F32)


def tn(a, b):
    return lax.dot_general(a, b, (((0,), (0,)), ((), ())), preferred_element_type=F32)


def attention_kernel(qkv_ref, d_ref, att_ref, dqkv_ref, dk_acc, dv_acc):
    cells = qkv_ref.shape[0]
    lane = lax.broadcasted_iota(jnp.int32, (1, PAIR), 1)
    keep = [lane < PAIR // 2, lane >= PAIR // 2]
    dk_acc[...] = jnp.zeros_like(dk_acc)
    dv_acc[...] = jnp.zeros_like(dv_acc)
    k = qkv_ref[:, PAIR : 2 * PAIR]
    v = qkv_ref[:, 2 * PAIR :]

    @pl.loop(0, cells // BLOCK)
    def _(step):
        rows = pl.ds(pl.multiple_of(step * BLOCK, BLOCK), BLOCK)
        q = qkv_ref[rows, :PAIR] * jnp.bfloat16(0.125)
        d = d_ref[rows, :]
        zero = jnp.zeros_like(q)
        att, dq = jnp.zeros((BLOCK, PAIR), F32), jnp.zeros((BLOCK, PAIR), F32)
        dk, dv = dk_acc[...], dv_acc[...]
        for mine in keep:
            qh = jnp.where(mine, q, zero)
            dh = jnp.where(mine, d, zero)
            scores = nt(qh, k)
            e = jnp.exp(scores - jnp.max(scores, -1, keepdims=True))
            p = e * (1.0 / jnp.sum(e, -1, keepdims=True))
            pb = p.astype(BF16)
            o = jnp.dot(pb, v, preferred_element_type=F32).astype(BF16).astype(F32)
            att = jnp.where(mine, o, att)
            delta = jnp.sum(dh.astype(F32) * o, -1, keepdims=True)
            ds = (p * (nt(dh, v) - delta)).astype(BF16)
            dq = jnp.where(mine, jnp.dot(ds, k, preferred_element_type=F32), dq)
            dk = dk + tn(ds, qh)
            dv = dv + tn(pb, dh)
        dk_acc[...] = dk
        dv_acc[...] = dv
        att_ref[rows, :] = att.astype(BF16)
        dqkv_ref[rows, :PAIR] = (0.125 * dq).astype(BF16)

    dqkv_ref[:, PAIR : 2 * PAIR] = dk_acc[...].astype(BF16)
    dqkv_ref[:, 2 * PAIR :] = dv_acc[...].astype(BF16)


def attention(qkv, d_att):
    cells = qkv.shape[0]
    return pl.pallas_call(
        attention_kernel,
        out_shape=(
            jax.ShapeDtypeStruct((cells, PAIR), BF16),
            jax.ShapeDtypeStruct((cells, 3 * PAIR), BF16),
        ),
        scratch_shapes=[pltpu.VMEM((cells, PAIR), F32)] * 2,
        compiler_params=pltpu.CompilerParams(vmem_limit_bytes=48 * 2**20),
        cost_estimate=pl.CostEstimate(
            flops=2 * 6 * 2 * cells * cells * PAIR, bytes_accessed=2**21, transcendentals=2 * cells * cells
        ),
    )(qkv, d_att)


def turn(x, by):
    pairs = [(z * 2 + c, (z + by) % Z * 2 + c) for z in range(Z) for c in range(2)]
    return lax.ppermute(x, "space", pairs)


def swap(x):
    return lax.ppermute(x, "space", [(i, i ^ 1) for i in range(2 * Z)])


def transpose_devices(x):
    at = lambda t, y, s: (t * 4 + y) * 8 + s
    pairs = [(at(t, y, s), at(s, y, t)) for t in range(8) for y in range(4) for s in range(8)]
    return lax.ppermute(x, ("dp", "space"), pairs)


def gather_cells(x):
    mine = jnp.concatenate([x] + [turn(x, by) for by in range(1, Z)], 0)
    return jnp.concatenate([mine, swap(mine)], 0)


def body(images, cotangent, w_qkv, w_out, film, timesteps):
    rows = images.shape[1]
    place = lax.axis_index("space")
    w_rows = w_qkv.shape[0]
    w_part = lax.dynamic_slice_in_dim(w_qkv.reshape(w_rows, 3, 8, PAIR), place, 1, 2)
    w_part = w_part.reshape(w_rows, 3 * PAIR)
    o_part = transpose_devices(lax.dynamic_slice_in_dim(w_out, place * PAIR, PAIR, 1))
    part = jnp.concatenate([w_part, o_part], 1)
    parts = lax.all_to_all(
        jnp.broadcast_to(part[None], (32,) + part.shape), "dp", 0, 0, tiled=True
    )
    wq = parts[..., : 3 * PAIR].reshape(C, 3 * PAIR)
    wo = parts[..., 3 * PAIR :].reshape(8, 4 * w_rows, PAIR)
    wo = jnp.transpose(wo, (1, 0, 2)).reshape(4 * w_rows, C)

    feature_row = lax.dynamic_slice_in_dim(film, timesteps[0], 1, 0).astype(F32)
    xf = images[0].astype(F32)
    mean_x = jnp.mean(xf, -1, keepdims=True)
    centered = xf - mean_x
    inverse = lax.rsqrt(jnp.mean(centered * centered, -1, keepdims=True) + 1e-05)
    xhat = centered * inverse
    scale = 1.0 + feature_row[:, :C]
    normed = (xhat * scale + feature_row[:, C:]).astype(BF16)
    normed_all = gather_cells(normed)
    cot_all = gather_cells(cotangent[0])

    qkv = jnp.dot(normed_all, wq, preferred_element_type=F32).astype(BF16)
    d_att = nt(cot_all, wo).astype(BF16)
    att, dqkv = attention(qkv, d_att)

    partial = nt(dqkv, wq).astype(BF16)
    half = Z * rows
    chip = partial[:half].astype(F32) + swap(partial[half:]).astype(F32)
    dnormed = chip[:rows]
    for by in range(1, Z):
        dnormed = dnormed + turn(chip[by * rows : (by + 1) * rows].astype(BF16), Z - by).astype(F32)
    dxhat = dnormed * scale
    branch = inverse * (
        dxhat
        - jnp.mean(dxhat, -1, keepdims=True)
        - xhat * jnp.mean(dxhat * xhat, -1, keepdims=True)
    )

    gq = tn(normed_all, dqkv).astype(BF16).reshape(32, w_rows, 3 * PAIR)
    go = tn(att, cot_all).astype(BF16).reshape(4 * w_rows, 8, PAIR)
    go = jnp.transpose(go, (1, 0, 2)).reshape(32, w_rows, PAIR)
    sent = lax.all_to_all(jnp.concatenate([gq, go], -1), "dp", 0, 0, tiled=True)
    total = jnp.sum(sent.astype(F32), 0).astype(BF16)
    mine = jnp.concatenate([total[:, : 3 * PAIR], transpose_devices(total[:, 3 * PAIR :])], 1)
    every = lax.all_gather(mine, "space", axis=0, tiled=False).astype(F32)
    every = jnp.transpose(every.reshape(8, w_rows, 4, PAIR), (1, 2, 0, 3))
    grad_q = every[:, :3].reshape(w_rows, 3 * C)
    grad_o = every[:, 3].reshape(w_rows, C)
    return branch.astype(BF16)[None], grad_q, grad_o


def solution(mesh):
    return jax.shard_map(
        body,
        mesh=mesh,
        in_specs=(
            P("dp", "space", None),
            P("dp", "space", None),
            P("dp", None),
            P("dp", None),
            P(),
            P("dp"),
        ),
        out_specs=(P("dp", "space", None), P("dp", None), P("dp", None)),
        check_vma=False,
    )
```

```python
import jax
import jax.numpy as jnp
from jax import lax
from jax.experimental import pallas as pl
from jax.experimental.pallas import tpu as pltpu
from jax.sharding import PartitionSpec as P

C = 1024
Z = 4
XY = 16
ROWS = 32
CELLS = 128
PAIR = 128
QKV = 3 * PAIR
PIECES = 10
BLOCK = 256
F32 = jnp.float32
BF16 = jnp.bfloat16
FAR = pl.BlockSpec(memory_space=pltpu.HBM)
WHOLE = pl.BlockSpec(memory_space=pltpu.VMEM)
SCALARS = pl.BlockSpec(memory_space=pltpu.SMEM)
CHEAP = pl.CostEstimate(flops=0, bytes_accessed=0, transcendentals=0)
SMALL = pltpu.CompilerParams(vmem_limit_bytes=8 * 2**20)
PARAMS = pltpu.CompilerParams(vmem_limit_bytes=58 * 2**20)


def nt(a, b):
    return lax.dot_general(a, b, (((1,), (1,)), ((), ())), preferred_element_type=F32)


def tn(a, b):
    return lax.dot_general(a, b, (((0,), (0,)), ((), ())), preferred_element_type=F32)


def nn(a, b):
    return jnp.dot(a, b, preferred_element_type=F32)


def struct(shape, dtype=BF16):
    return jax.ShapeDtypeStruct(shape, dtype)


def heads():
    lane = lax.broadcasted_iota(jnp.int32, (1, PAIR), 1)
    return lane < PAIR // 2, lane >= PAIR // 2


def load(pieces, whole, sems):
    copies, at = [], 0
    for i, piece in enumerate(pieces):
        rows = piece.shape[0]
        copies.append(pltpu.make_async_copy(piece, whole.at[at : at + rows, :], sems.at[i]))
        at += rows
    for copy in copies:
        copy.start()
    return copies


def attention_kernel(where, *refs):
    pieces, parts, rest = refs[:PIECES], refs[PIECES : PIECES + 4], refs[PIECES + 4 :]
    dqkv, wq, sent, x, qkv, wo, att, d_att, dk_acc, dv_acc, sems = rest
    copies = load(pieces, x, sems)
    for far, part in enumerate(parts):
        col = lax.rem(where[2] - far + 4, 4)
        for lo in range(2):
            half = slice(lo * ROWS, (lo + 1) * ROWS)
            columns = pl.ds(pl.multiple_of((lo * 4 + col) * PAIR, PAIR), PAIR)
            for y in range(4):
                at = pl.multiple_of(((lo * 4 + col) * 4 + y) * ROWS, ROWS)
                wq[pl.ds(at, ROWS), :] = part[y, half, :QKV]
                wo[y * ROWS : (y + 1) * ROWS, columns] = part[y, half, QKV:]
    for copy in copies:
        copy.wait()
    qkv[...] = nn(x[:, :C], wq[...]).astype(BF16)
    d_att[...] = nt(x[:, C:], wo[...]).astype(BF16)
    dk_acc[...] = jnp.zeros_like(dk_acc)
    dv_acc[...] = jnp.zeros_like(dv_acc)
    k = qkv[:, PAIR : 2 * PAIR]
    v = qkv[:, 2 * PAIR :]

    @pl.loop(0, qkv.shape[0] // BLOCK)
    def _(step):
        rows = pl.ds(pl.multiple_of(step * BLOCK, BLOCK), BLOCK)
        q = qkv[rows, :PAIR] * jnp.bfloat16(0.125)
        d = d_att[rows, :]
        zero = jnp.zeros_like(q)
        a, dq = jnp.zeros((BLOCK, PAIR), F32), jnp.zeros((BLOCK, PAIR), F32)
        dk, dv = dk_acc[...], dv_acc[...]
        for mine in heads():
            qh = jnp.where(mine, q, zero)
            dh = jnp.where(mine, d, zero)
            scores = nt(qh, k)
            e = jnp.exp(scores - jnp.max(scores, -1, keepdims=True))
            p = e * (1.0 / jnp.sum(e, -1, keepdims=True))
            pb = p.astype(BF16)
            o = nn(pb, v).astype(BF16).astype(F32)
            a = jnp.where(mine, o, a)
            delta = jnp.sum(dh.astype(F32) * o, -1, keepdims=True)
            ds = (p * (nt(dh, v) - delta)).astype(BF16)
            dq = jnp.where(mine, nn(ds, k), dq)
            dk = dk + tn(ds, qh)
            dv = dv + tn(pb, dh)
        dk_acc[...] = dk
        dv_acc[...] = dv
        att[rows, :] = a.astype(BF16)
        dqkv[rows, :PAIR] = (0.125 * dq).astype(BF16)

    dqkv[:, PAIR : 2 * PAIR] = dk_acc[...].astype(BF16)
    dqkv[:, 2 * PAIR :] = dv_acc[...].astype(BF16)
    grad = tn(x[:, :C], dqkv[...]).astype(BF16)
    for lo in range(2):
        for xy in range(XY):
            at = (lo * XY + xy) * ROWS
            sent[xy, lo * ROWS : (lo + 1) * ROWS, :QKV] = grad[at : at + ROWS, :]
    grad = tn(att[...], x[:, C:]).astype(BF16)
    for xy in range(XY):
        x, y = divmod(xy, 4)
        for lo in range(2):
            at = (lo * 4 + x) * PAIR
            sent[xy, lo * ROWS : (lo + 1) * ROWS, QKV:] = grad[
                y * ROWS : (y + 1) * ROWS, at : at + PAIR
            ]


def attention(where, pieces, parts):
    cells = 8 * CELLS
    return pl.pallas_call(
        attention_kernel,
        in_specs=[SCALARS] + [FAR] * PIECES + [WHOLE] * 4,
        out_shape=(
            struct((cells, QKV)),
            struct((C, QKV)),
            struct((XY, 2 * ROWS, QKV + PAIR)),
        ),
        scratch_shapes=[
            pltpu.VMEM((cells, 2 * C), BF16),
            pltpu.VMEM((cells, QKV), BF16),
            pltpu.VMEM((PAIR, C), BF16),
            pltpu.VMEM((cells, PAIR), BF16),
            pltpu.VMEM((cells, PAIR), BF16),
            pltpu.VMEM((cells, PAIR), F32),
            pltpu.VMEM((cells, PAIR), F32),
            pltpu.SemaphoreType.DMA((PIECES,)),
        ],
        compiler_params=PARAMS,
        cost_estimate=pl.CostEstimate(
            flops=2**34, bytes_accessed=2**23, transcendentals=2 * cells * cells
        ),
    )(where, *pieces, *parts)


def dnormed_kernel(dqkv, wq, out, *mine):
    half = Z * CELLS
    out[...] = nt(dqkv[half:, :], wq[...]).astype(BF16)
    for i, piece in enumerate(mine):
        piece[...] = nt(dqkv[i * CELLS : (i + 1) * CELLS, :], wq[...]).astype(BF16)


def dnormed_terms(dqkv, wq):
    return pl.pallas_call(
        dnormed_kernel,
        out_shape=(struct((Z * CELLS, C)), *[struct((CELLS, C))] * Z),
        compiler_params=PARAMS,
        cost_estimate=CHEAP,
    )(dqkv, wq)


def normalize(image, row):
    xf = image.astype(F32)
    centered = xf - jnp.mean(xf, -1, keepdims=True)
    inverse = lax.rsqrt(jnp.mean(centered * centered, -1, keepdims=True) + 1e-05)
    return centered * inverse, inverse, 1.0 + row[:, :C].astype(F32)


def prepare_kernel(where, image, cot, row, w_qkv, w_out, x, w_part, o_part):
    xhat, _, scale = normalize(image[...], row[...])
    x[:, :C] = (xhat * scale + row[:, C:].astype(F32)).astype(BF16)
    x[:, C:] = cot[...]
    for part in range(3):
        at = pl.multiple_of(part * C + where[0] * PAIR, PAIR)
        w_part[:, part * PAIR : (part + 1) * PAIR] = w_qkv[:, pl.ds(at, PAIR)]
    for lo in range(2):
        at = pl.multiple_of(lo * 4 * PAIR + lax.rem(where[0], 4) * PAIR, PAIR)
        o_part[lo * ROWS : (lo + 1) * ROWS, :] = w_out[:, pl.ds(at, PAIR)]


def prepare(where, image, cot, row, w_qkv, w_out):
    return pl.pallas_call(
        prepare_kernel,
        in_specs=[SCALARS] + [WHOLE] * 5,
        out_shape=(
            struct((CELLS, 2 * C)),
            struct((ROWS, QKV)),
            struct((2 * ROWS, PAIR)),
        ),
        cost_estimate=CHEAP,
        compiler_params=PARAMS,
    )(where, image, cot, row, w_qkv, w_out)


def pack_kernel(where, w_part, w_far, o_part, packed):
    low = where[1] == 0
    near, far = w_part[...], w_far[...]
    packed[:ROWS, :QKV] = jnp.where(low, near, far)
    packed[ROWS:, :QKV] = jnp.where(low, far, near)
    packed[:, QKV:] = o_part[...]


def pack(where, w_part, w_far, o_part):
    return pl.pallas_call(
        pack_kernel,
        in_specs=[SCALARS] + [WHOLE] * 3,
        out_shape=struct((2 * ROWS, QKV + PAIR)),
        cost_estimate=CHEAP,
        compiler_params=SMALL,
    )(where, w_part, w_far, o_part)


def join_kernel(where, *refs):
    pieces, joined = refs[:-1], refs[-1]
    for far, piece in enumerate(pieces):
        joined[lax.rem(where[3] - far + 4, 4)] = piece[...]


def join(where, pieces):
    return pl.pallas_call(
        join_kernel,
        in_specs=[SCALARS] + [WHOLE] * 4,
        out_shape=struct((4, 2 * ROWS, QKV + PAIR)),
        cost_estimate=CHEAP,
        compiler_params=SMALL,
    )(where, *pieces)


def total_kernel(where, sent, near, far, go):
    total = sent[0].astype(F32)
    for xy in range(1, XY):
        total = total + sent[xy].astype(F32)
    go[...] = total[:, QKV:].astype(BF16)
    low = where[1] == 0
    first, second = total[:ROWS, :QKV], total[ROWS:, :QKV]
    near[...] = jnp.where(low, first, second)
    far[...] = jnp.where(low, second, first).astype(BF16)


def add_up(where, sent):
    return pl.pallas_call(
        total_kernel,
        in_specs=[SCALARS, WHOLE],
        out_shape=(struct((ROWS, QKV), F32), struct((ROWS, QKV)), struct((2 * ROWS, PAIR))),
        cost_estimate=CHEAP,
        compiler_params=SMALL,
    )(where, sent)


def finish_kernel(image, row, *refs):
    pieces, branch = refs[:-1], refs[-1]
    xhat, inverse, scale = normalize(image[...], row[...])
    dnormed = pieces[0][...].astype(F32)
    for piece in pieces[1:]:
        dnormed = dnormed + piece[...].astype(F32)
    dxhat = dnormed * scale
    mean = jnp.mean(dxhat, -1, keepdims=True)
    along = jnp.mean(dxhat * xhat, -1, keepdims=True)
    branch[...] = (inverse * (dxhat - mean - xhat * along)).astype(BF16)


def finish(image, row, pieces):
    return pl.pallas_call(
        finish_kernel,
        out_shape=struct((CELLS, C)),
        in_specs=[WHOLE] * (2 + len(pieces)),
        cost_estimate=CHEAP,
        compiler_params=SMALL,
    )(image, row, *pieces)


def place_kernel(where, near, other, grad_q, grad_o):
    pieces = [near.at[i] for i in range(Z)] + [other.at[i] for i in range(Z)]
    z, core = where[0] // 2, lax.rem(where[0], 2)
    lane = lax.broadcasted_iota(jnp.int32, (1, 4 * PAIR), 1) // PAIR
    halves = [jnp.zeros((ROWS, 4 * PAIR), F32), jnp.zeros((ROWS, 4 * PAIR), F32)]
    for i, piece in enumerate(pieces):
        far, other = i % 4, i // 4
        place = (z ^ far) * 2 + (core if other == 0 else 1 - core)
        for part in range(3):
            at = pl.multiple_of(part * C + place * PAIR, PAIR)
            grad_q[:, pl.ds(at, PAIR)] = piece[:, part * PAIR : (part + 1) * PAIR].astype(F32)
        mine = lane == lax.rem(place, 4)
        for lo in range(2):
            at = QKV + lo * PAIR
            value = piece[:, at : at + PAIR].astype(F32)
            halves[lo] = halves[lo] + jnp.where(mine, jnp.concatenate([value] * 4, 1), 0.0)
    grad_o[:, : 4 * PAIR] = halves[0]
    grad_o[:, 4 * PAIR :] = halves[1]


def place(near, other, where):
    return pl.pallas_call(
        place_kernel,
        in_specs=[SCALARS] + [WHOLE] * 2,
        out_shape=(struct((ROWS, 3 * C), F32), struct((ROWS, C), F32)),
        cost_estimate=CHEAP,
        compiler_params=SMALL,
    )(where, near, other)


def turn(x, by):
    pairs = [(z * 2 + c, (z + by) % Z * 2 + c) for z in range(Z) for c in range(2)]
    return lax.ppermute(x, "space", pairs)


def swap(x):
    return lax.ppermute(x, "space", [(i, i ^ 1) for i in range(2 * Z)])


def swap_lo(x):
    return lax.ppermute(x, "dp", [(i, i ^ XY) for i in range(2 * XY)])


def transpose_devices(x):
    at = lambda t, y, s: (t * 4 + y) * 8 + s
    pairs = [(at(t, y, s), at(s, y, t)) for t in range(8) for y in range(4) for s in range(8)]
    return lax.ppermute(x, ("dp", "space"), pairs)


def turn_dp(x, by_x, by_y):
    at = lambda lo, col, y: (lo * 4 + col % 4) * 4 + y % 4
    pairs = [
        (at(lo, col, y), at(lo, col + by_x, y + by_y))
        for lo in range(2)
        for col in range(4)
        for y in range(4)
    ]
    return lax.ppermute(x, "dp", pairs)


def over_xy(x):
    groups = [list(range(XY)), list(range(XY, 2 * XY))]
    return lax.all_to_all(x, "dp", 0, 0, axis_index_groups=groups, tiled=True)


def meet(x, by):
    pairs = [(z * 2 + c, (z ^ by) * 2 + c) for z in range(Z) for c in range(2)]
    return lax.ppermute(x, "space", pairs)


def after(x, *others):
    return lax.optimization_barrier((x, others))[0]


def body(images, cotangent, w_qkv, w_out, film, timesteps):
    space, dp = lax.axis_index("space"), lax.axis_index("dp")
    where = jnp.stack([space, dp // XY, lax.rem(dp // 4, 4), lax.rem(dp, 4)])
    row = lax.dynamic_slice_in_dim(film, timesteps[0], 1, 0)
    image = images[0]
    x, w_part, o_part = prepare(where, image, cotangent[0], row, w_qkv, w_out)
    w_far, o_part = swap_lo(w_part), transpose_devices(o_part)
    x = after(x, w_far, o_part)
    one, three = turn(x, 1), turn(x, 3)
    packed = pack(where, w_part, w_far, o_part)
    packed = [packed] + [turn_dp(packed, 0, by) for by in range(1, 4)]
    parts = join(where, packed)
    parts = [parts] + [turn_dp(parts, by, 0) for by in range(1, 4)]
    half = CELLS // 2
    two = turn(after(one[:half], *packed), 1), turn(after(three[half:], *packed), 3)
    pieces = [after(x, *parts), after(one, *parts), *two, after(three, *parts)]
    pieces += [swap(piece) for piece in pieces]
    dqkv, wq, grads = attention(where, pieces, parts)
    grads = over_xy(grads)

    out, *mine = dnormed_terms(dqkv, wq)
    other = swap(out)
    sums = [
        (piece.astype(F32) + other[i * CELLS : (i + 1) * CELLS].astype(F32)).astype(BF16)
        for i, piece in enumerate(mine)
    ]
    own, one, two, three = sums[0], turn(sums[1], 3), turn(sums[2], 2), turn(sums[3], 1)

    near, far, go = add_up(where, after(grads, one, two, three))
    go = transpose_devices(go)
    gq = (near + swap_lo(far).astype(F32)).astype(BF16)
    mine = jnp.concatenate([gq, go[:ROWS], go[ROWS:]], 1)
    every = jnp.stack([mine, meet(mine, 1)])
    every = jnp.concatenate([every, meet(every, 2)], 0)
    grad_q, grad_o = place(every, swap(every), where)
    branch = finish(image, row, (own, one, two, three))
    return branch[None], grad_q, grad_o


def solution(mesh):
    return jax.shard_map(
        body,
        mesh=mesh,
        in_specs=(
            P("dp", "space", None),
            P("dp", "space", None),
            P("dp", None),
            P("dp", None),
            P(),
            P("dp"),
        ),
        out_specs=(P("dp", "space", None), P("dp", None), P("dp", None)),
        check_vma=False,
    )
```

```python
import jax
import jax.numpy as jnp
from jax import lax
from jax.experimental import pallas as pl
from jax.experimental.pallas import tpu as pltpu
from jax.sharding import PartitionSpec as P

C = 1024
Z = 4
XY = 16
ROWS = 32
CELLS = 128
PAIR = 128
QKV = 3 * PAIR
PIECES = 10
F32 = jnp.float32
BF16 = jnp.bfloat16
FAR = pl.BlockSpec(memory_space=pltpu.HBM)
WHOLE = pl.BlockSpec(memory_space=pltpu.VMEM)
SCALARS = pl.BlockSpec(memory_space=pltpu.SMEM)
CHEAP = pl.CostEstimate(flops=0, bytes_accessed=0, transcendentals=0)
SMALL = pltpu.CompilerParams(vmem_limit_bytes=8 * 2**20)
PARAMS = pltpu.CompilerParams(vmem_limit_bytes=58 * 2**20)


def nt(a, b):
    return lax.dot_general(a, b, (((1,), (1,)), ((), ())), preferred_element_type=F32)


def tn(a, b):
    return lax.dot_general(a, b, (((0,), (0,)), ((), ())), preferred_element_type=F32)


def nn(a, b):
    return jnp.dot(a, b, preferred_element_type=F32)


def struct(shape, dtype=BF16):
    return jax.ShapeDtypeStruct(shape, dtype)


def heads():
    lane = lax.broadcasted_iota(jnp.int32, (1, PAIR), 1)
    return lane < PAIR // 2, lane >= PAIR // 2


def attention_kernel(where, *refs):
    pieces, parts, rest = refs[:PIECES], refs[PIECES : PIECES + 4], refs[PIECES + 4 :]
    grads, *results = rest[:7]
    x, weights, wq, wo, qkv, att, d_att, dqkv, turned, sent, terms, sems = rest[7:]
    copies, at = [], 0
    for i, part in enumerate(parts):
        copies.append(pltpu.make_async_copy(part, weights.at[i], sems.at[PIECES + i]))
    for i, piece in enumerate(pieces):
        to = x.at[at : at + piece.shape[0], :]
        copies.append(pltpu.make_async_copy(piece, to, sems.at[i]))
        at += piece.shape[0]
    for copy in copies:
        copy.start()
    for far in range(4):
        copies[far].wait()
        col = lax.rem(where[2] - far + 4, 4)
        for lo in range(2):
            half = slice(lo * ROWS, (lo + 1) * ROWS)
            columns = pl.ds(pl.multiple_of((lo * 4 + col) * PAIR, PAIR), PAIR)
            for y in range(4):
                at = pl.multiple_of(((lo * 4 + col) * 4 + y) * ROWS, ROWS)
                wq[pl.ds(at, ROWS), :] = weights[far, y, half, :QKV]
                wo[y * ROWS : (y + 1) * ROWS, columns] = weights[far, y, half, QKV:]
    cells = Z * CELLS
    for core in range(2):
        rows = slice(core * cells, (core + 1) * cells)
        for copy in copies[4 + core * PIECES // 2 : 4 + (core + 1) * PIECES // 2]:
            copy.wait()
        qkv[rows, :] = nn(x[rows, :C], wq[...]).astype(BF16)
        d_att[rows, :] = nt(x[rows, C:], wo[...]).astype(BF16)
    q = qkv[:, :PAIR] * jnp.bfloat16(0.125)
    k = qkv[:, PAIR : 2 * PAIR]
    v = qkv[:, 2 * PAIR :]
    d = d_att[...]
    zero = jnp.zeros_like(q)
    for head, mine_head in enumerate(heads()):
        qh = jnp.where(mine_head, q, zero)
        dh = jnp.where(mine_head, d, zero)
        scores = nt(qh, k)
        e = jnp.exp(scores - jnp.max(scores, -1, keepdims=True))
        p = e * (1.0 / jnp.sum(e, -1, keepdims=True))
        pb = p.astype(BF16)
        o = nn(pb, v).astype(BF16).astype(F32)
        delta = jnp.sum(dh.astype(F32) * o, -1, keepdims=True)
        ds = (p * (nt(dh, v) - delta)).astype(BF16)
        dq = (0.125 * nn(ds, k)).astype(BF16)
        dk, dv = tn(qh, ds), tn(dh, pb)
        if head == 0:
            att[...] = o.astype(BF16)
            dqkv[:, :PAIR] = dq
            turned[:PAIR, :] = dk
            turned[PAIR:, :] = dv
        else:
            att[...] = jnp.where(mine_head, o.astype(BF16), att[...])
            dqkv[:, :PAIR] = jnp.where(mine_head, dq, dqkv[:, :PAIR])
            turned[:PAIR, :] += dk
            turned[PAIR:, :] += dv

    dqkv[:, PAIR:] = turned[...].T.astype(BF16)
    grad = tn(dqkv[...], x[:, :C]).T.astype(BF16)
    for lo in range(2):
        for xy in range(XY):
            at = (lo * XY + xy) * ROWS
            sent[xy, lo * ROWS : (lo + 1) * ROWS, :QKV] = grad[at : at + ROWS, :]
    grad = tn(att[...], x[:, C:]).astype(BF16)
    for xy in range(XY):
        col, y = divmod(xy, 4)
        for lo in range(2):
            at = (lo * 4 + col) * PAIR
            sent[xy, lo * ROWS : (lo + 1) * ROWS, QKV:] = grad[
                y * ROWS : (y + 1) * ROWS, at : at + PAIR
            ]
    copies = [pltpu.make_async_copy(sent, grads, sems.at[0])]
    copies[0].start()
    far, near = results[0], results[1]
    order = [(Z + 2, far)]
    order += [(Z + spot, near.at[i * CELLS : (i + 1) * CELLS]) for i, spot in enumerate((0, 1, 3))]
    order += list(zip((2, 0, 1, 3), results[2:]))
    for i, (spot, to) in enumerate(order):
        rows = slice(spot * CELLS, (spot + 1) * CELLS)
        terms[rows, :] = nt(dqkv[rows, :], wq[...]).astype(BF16)
        copies.append(pltpu.make_async_copy(terms.at[rows, :], to, sems.at[i + 1]))
        copies[-1].start()
    for copy in copies:
        copy.wait()


def attention(where, pieces, parts):
    cells = 8 * CELLS
    return pl.pallas_call(
        attention_kernel,
        in_specs=[SCALARS] + [FAR] * (PIECES + 4),
        out_specs=[FAR] * 7,
        out_shape=(
            struct((XY, 2 * ROWS, QKV + PAIR)),
            struct((CELLS, C)),
            struct((3 * CELLS, C)),
            *[struct((CELLS, C))] * Z,
        ),
        scratch_shapes=[
            pltpu.VMEM((cells, 2 * C), BF16),
            pltpu.VMEM((4, 4, 2 * ROWS, QKV + PAIR), BF16),
            pltpu.VMEM((C, QKV), BF16),
            pltpu.VMEM((PAIR, C), BF16),
            pltpu.VMEM((cells, QKV), BF16),
            pltpu.VMEM((cells, PAIR), BF16),
            pltpu.VMEM((cells, PAIR), BF16),
            pltpu.VMEM((cells, QKV), BF16),
            pltpu.VMEM((2 * PAIR, cells), F32),
            pltpu.VMEM((XY, 2 * ROWS, QKV + PAIR), BF16),
            pltpu.VMEM((cells, C), BF16),
            pltpu.SemaphoreType.DMA((PIECES + 4,)),
        ],
        compiler_params=PARAMS,
        cost_estimate=pl.CostEstimate(
            flops=2**34, bytes_accessed=2**23, transcendentals=2 * cells * cells
        ),
    )(where, *pieces, *parts)


def normalize(image, row):
    xf = image.astype(F32)
    centered = xf - jnp.mean(xf, -1, keepdims=True)
    inverse = lax.rsqrt(jnp.mean(centered * centered, -1, keepdims=True) + 1e-05)
    return centered * inverse, inverse, 1.0 + row[:, :C].astype(F32)


def prepare_kernel(image, cot, row, x):
    xhat, _, scale = normalize(image[...], row[...])
    x[:, :C] = (xhat * scale + row[:, C:].astype(F32)).astype(BF16)
    x[:, C:] = cot[...]


def prepare(image, cot, row):
    return pl.pallas_call(
        prepare_kernel,
        in_specs=[WHOLE] * 3,
        out_shape=struct((CELLS, 2 * C)),
        cost_estimate=CHEAP,
        compiler_params=PARAMS,
    )(image, cot, row)


def cut_kernel(w_qkv, w_out, w_part, o_part, sems):
    space = lax.axis_index("space")
    copies = []
    for part in range(3):
        at = pl.multiple_of(part * C + space * PAIR, PAIR)
        to = w_part.at[:, part * PAIR : (part + 1) * PAIR]
        copies.append(pltpu.make_async_copy(w_qkv.at[:, pl.ds(at, PAIR)], to, sems.at[part]))
    for lo in range(2):
        at = pl.multiple_of(lo * 4 * PAIR + lax.rem(space, 4) * PAIR, PAIR)
        to = o_part.at[lo * ROWS : (lo + 1) * ROWS, :]
        copies.append(pltpu.make_async_copy(w_out.at[:, pl.ds(at, PAIR)], to, sems.at[3 + lo]))
    for copy in copies:
        copy.start()
    for copy in copies:
        copy.wait()


def cut(w_qkv, w_out):
    return pl.pallas_call(
        cut_kernel,
        in_specs=[FAR] * 2,
        out_shape=(struct((ROWS, QKV)), struct((2 * ROWS, PAIR))),
        scratch_shapes=[pltpu.SemaphoreType.DMA((5,))],
        cost_estimate=CHEAP,
        compiler_params=PARAMS,
    )(w_qkv, w_out)


def pack_kernel(where, w_part, w_far, o_part, packed):
    low = where[1] == 0
    near, far = w_part[...], w_far[...]
    packed[:ROWS, :QKV] = jnp.where(low, near, far)
    packed[ROWS:, :QKV] = jnp.where(low, far, near)
    packed[:, QKV:] = o_part[...]


def pack(where, w_part, w_far, o_part):
    return pl.pallas_call(
        pack_kernel,
        in_specs=[SCALARS] + [WHOLE] * 3,
        out_shape=struct((2 * ROWS, QKV + PAIR)),
        cost_estimate=CHEAP,
        compiler_params=SMALL,
    )(where, w_part, w_far, o_part)


def join_kernel(where, *refs):
    pieces, joined = refs[:-1], refs[-1]
    for far, piece in enumerate(pieces):
        joined[lax.rem(where[3] - far + 4, 4)] = piece[...]


def join(where, pieces):
    return pl.pallas_call(
        join_kernel,
        in_specs=[SCALARS] + [WHOLE] * 4,
        out_shape=struct((4, 2 * ROWS, QKV + PAIR)),
        cost_estimate=CHEAP,
        compiler_params=SMALL,
    )(where, *pieces)


def total_kernel(where, sent, near, far, go):
    total = sent[0].astype(F32)
    for xy in range(1, XY):
        total = total + sent[xy].astype(F32)
    go[...] = total[:, QKV:].astype(BF16)
    low = where[1] == 0
    first, second = total[:ROWS, :QKV], total[ROWS:, :QKV]
    near[...] = jnp.where(low, first, second)
    far[...] = jnp.where(low, second, first).astype(BF16)


def add_up(where, sent):
    return pl.pallas_call(
        total_kernel,
        in_specs=[SCALARS, WHOLE],
        out_shape=(struct((ROWS, QKV), F32), struct((ROWS, QKV)), struct((2 * ROWS, PAIR))),
        cost_estimate=CHEAP,
        compiler_params=SMALL,
    )(where, sent)


def finish_kernel(image, row, *refs):
    pieces, branch = refs[:-1], refs[-1]
    xhat, inverse, scale = normalize(image[...], row[...])
    dnormed = pieces[0][...].astype(F32)
    for piece in pieces[1:]:
        dnormed = dnormed + piece[...].astype(F32)
    dxhat = dnormed * scale
    mean = jnp.mean(dxhat, -1, keepdims=True)
    along = jnp.mean(dxhat * xhat, -1, keepdims=True)
    branch[...] = (inverse * (dxhat - mean - xhat * along)).astype(BF16)


def finish(image, row, pieces):
    return pl.pallas_call(
        finish_kernel,
        out_shape=struct((CELLS, C)),
        in_specs=[WHOLE] * (2 + len(pieces)),
        cost_estimate=CHEAP,
        compiler_params=SMALL,
    )(image, row, *pieces)


def place_kernel(where, *refs):
    pieces, (grad_q, grad_o) = refs[:-2], refs[-2:]
    z, core = where[0] // 2, lax.rem(where[0], 2)
    lane = lax.broadcasted_iota(jnp.int32, (1, 4 * PAIR), 1) // PAIR
    halves = [jnp.zeros((ROWS, 4 * PAIR), F32), jnp.zeros((ROWS, 4 * PAIR), F32)]
    for i, piece in enumerate(pieces):
        far, other = i % 4, i // 4
        place = lax.rem(z - far + Z, Z) * 2 + (core if other == 0 else 1 - core)
        for part in range(3):
            at = pl.multiple_of(part * C + place * PAIR, PAIR)
            grad_q[:, pl.ds(at, PAIR)] = piece[:, part * PAIR : (part + 1) * PAIR].astype(F32)
        mine = lane == lax.rem(place, 4)
        for lo in range(2):
            at = QKV + lo * PAIR
            value = piece[:, at : at + PAIR].astype(F32)
            halves[lo] = halves[lo] + jnp.where(mine, jnp.concatenate([value] * 4, 1), 0.0)
    grad_o[:, : 4 * PAIR] = halves[0]
    grad_o[:, 4 * PAIR :] = halves[1]


def place(pieces, where):
    return pl.pallas_call(
        place_kernel,
        in_specs=[SCALARS] + [WHOLE] * 8,
        out_shape=(struct((ROWS, 3 * C), F32), struct((ROWS, C), F32)),
        cost_estimate=CHEAP,
        compiler_params=SMALL,
    )(where, *pieces)


def turn(x, by):
    pairs = [(z * 2 + c, (z + by) % Z * 2 + c) for z in range(Z) for c in range(2)]
    return lax.ppermute(x, "space", pairs)


def swap(x):
    return lax.ppermute(x, "space", [(i, i ^ 1) for i in range(2 * Z)])


def swap_lo(x):
    return lax.ppermute(x, "dp", [(i, i ^ XY) for i in range(2 * XY)])


def transpose_devices(x):
    at = lambda t, y, s: (t * 4 + y) * 8 + s
    pairs = [(at(t, y, s), at(s, y, t)) for t in range(8) for y in range(4) for s in range(8)]
    return lax.ppermute(x, ("dp", "space"), pairs)


def turn_dp(x, by_x, by_y):
    at = lambda lo, col, y: (lo * 4 + col % 4) * 4 + y % 4
    pairs = [
        (at(lo, col, y), at(lo, col + by_x, y + by_y))
        for lo in range(2)
        for col in range(4)
        for y in range(4)
    ]
    return lax.ppermute(x, "dp", pairs)


def over_xy(x):
    groups = [list(range(XY)), list(range(XY, 2 * XY))]
    return lax.all_to_all(x, "dp", 0, 0, axis_index_groups=groups, tiled=True)


def add(a, b):
    return (a.astype(F32) + b.astype(F32)).astype(BF16)


def after(x, *others):
    return lax.optimization_barrier((x, others))[0]


def body(images, cotangent, w_qkv, w_out, film, timesteps):
    space, dp = lax.axis_index("space"), lax.axis_index("dp")
    where = jnp.stack([space, dp // XY, lax.rem(dp // 4, 4), lax.rem(dp, 4)])
    row = lax.dynamic_slice_in_dim(film, timesteps[0], 1, 0)
    image = images[0]
    w_part, o_part = cut(w_qkv, w_out)
    w_far, o_part = swap_lo(w_part), transpose_devices(o_part)
    x = prepare(image, cotangent[0], row)
    x = after(x, w_far, o_part)
    one, three = turn(x, 1), turn(x, 3)
    packed = pack(where, w_part, w_far, o_part)
    packed = [packed] + [turn_dp(packed, 0, by) for by in range(1, 4)]
    parts = join(where, packed)
    x = after(x, *packed)
    parts = [parts] + [turn_dp(parts, by, 0) for by in range(1, 4)]
    one, three = after((one, three), parts[1], parts[2])
    half = CELLS // 2
    pieces = [x, one, turn(one[:half], 1), turn(three[half:], 3), three]
    pieces += [swap(piece) for piece in pieces]
    grads, far, near, two, own, one, three = attention(where, pieces, parts)
    grads = over_xy(grads)

    two = add(two, swap(far))
    near = swap(near)
    own, one, three = (
        add(piece, near[i * CELLS : (i + 1) * CELLS]) for i, piece in enumerate((own, one, three))
    )
    two = turn(two, 2)

    near, far, go = add_up(where, after(grads, two))
    go = transpose_devices(go)
    gq = (near + swap_lo(far).astype(F32)).astype(BF16)
    mine = jnp.concatenate([gq, go[:ROWS], go[ROWS:]], 1)
    one, three = turn(after(one, mine), 3), turn(after(three, mine), 1)
    every = [mine] + [turn(mine, by) for by in range(1, Z)]
    grad_q, grad_o = place(every + [swap(piece) for piece in every], where)
    branch = finish(image, row, (own, one, two, three))
    return branch[None], grad_q, grad_o


def solution(mesh):
    return jax.shard_map(
        body,
        mesh=mesh,
        in_specs=(
            P("dp", "space", None),
            P("dp", "space", None),
            P("dp", None),
            P("dp", None),
            P(),
            P("dp"),
        ),
        out_specs=(P("dp", "space", None), P("dp", None), P("dp", None)),
        check_vma=False,
    )
```

```python
import jax
import jax.numpy as jnp
from jax import lax
from jax.experimental import pallas as pl
from jax.experimental.pallas import tpu as pltpu
from jax.sharding import PartitionSpec as P

C = 1024
Z = 4
XY = 16
ROWS = 32
CELLS = 128
PAIR = 128
QKV = 3 * PAIR
PIECES = 10
F32 = jnp.float32
BF16 = jnp.bfloat16
FAR = pl.BlockSpec(memory_space=pltpu.HBM)
WHOLE = pl.BlockSpec(memory_space=pltpu.VMEM)
SCALARS = pl.BlockSpec(memory_space=pltpu.SMEM)
CHEAP = pl.CostEstimate(flops=0, bytes_accessed=0, transcendentals=0)
SMALL = pltpu.CompilerParams(vmem_limit_bytes=8 * 2**20)
PARAMS = pltpu.CompilerParams(vmem_limit_bytes=58 * 2**20)


def nt(a, b):
    return lax.dot_general(a, b, (((1,), (1,)), ((), ())), preferred_element_type=F32)


def tn(a, b):
    return lax.dot_general(a, b, (((0,), (0,)), ((), ())), preferred_element_type=F32)


def nn(a, b):
    return jnp.dot(a, b, preferred_element_type=F32)


def struct(shape, dtype=BF16):
    return jax.ShapeDtypeStruct(shape, dtype)


def heads():
    lane = lax.broadcasted_iota(jnp.int32, (1, PAIR), 1)
    return lane < PAIR // 2, lane >= PAIR // 2


def project_kernel(where, *refs):
    pieces, parts, (qkvd, wq, wo, x) = refs[:6], refs[6:10], refs[10:]
    for far, part in enumerate(parts):
        col = lax.rem(where[2] - far + 4, 4)
        for lo in range(2):
            half = slice(lo * ROWS, (lo + 1) * ROWS)
            columns = pl.ds(pl.multiple_of((lo * 4 + col) * PAIR, PAIR), PAIR)
            for y in range(4):
                at = pl.multiple_of(((lo * 4 + col) * 4 + y) * ROWS, ROWS)
                wq[pl.ds(at, ROWS), :] = part[y, half, :QKV]
                wo[y * ROWS : (y + 1) * ROWS, columns] = part[y, half, QKV:]
    for i, piece in enumerate(pieces):
        x[i * CELLS : (i + 1) * CELLS, :] = piece[...]
    qkvd[:, :QKV] = nn(x[:, :C], wq[...]).astype(BF16)
    qkvd[:, QKV:] = nt(x[:, C:], wo[...]).astype(BF16)


def project(where, pieces, parts):
    return pl.pallas_call(
        project_kernel,
        in_specs=[SCALARS] + [WHOLE] * 10,
        out_shape=(struct((6 * CELLS, QKV + PAIR)), struct((C, QKV)), struct((PAIR, C))),
        scratch_shapes=[pltpu.VMEM((6 * CELLS, 2 * C), BF16)],
        compiler_params=PARAMS,
        cost_estimate=CHEAP,
    )(where, *pieces, *parts)


def attention_kernel(*refs):
    pieces, rest = refs[:PIECES], refs[PIECES:]
    first, wq_far, wo_far, grads, *results = rest[:10]
    x, wq, wo, qkv, att, dqkv, turned, sent, terms, sems = rest[10:]
    starts = (0, 128, 256, 320, 384, 512, 640, 768, 832, 896)
    late = (2, 3, 7, 8)
    copies = [pltpu.make_async_copy(wq_far, wq, sems.at[PIECES])]
    copies.append(pltpu.make_async_copy(wo_far, wo, sems.at[PIECES + 1]))
    for i in late:
        to = x.at[starts[i] : starts[i] + pieces[i].shape[0], :]
        copies.append(pltpu.make_async_copy(pieces[i], to, sems.at[i]))
    for i, (at, to, size) in enumerate(
        ((0, 0, 256), (256, 384, 128), (384, 512, 256), (640, 896, 128))
    ):
        source = first.at[at : at + size, :]
        copies.append(
            pltpu.make_async_copy(source, qkv.at[to : to + size, :], sems.at[PIECES + 2 + i])
        )
    rest_of_x = []
    for i in range(PIECES):
        if i not in late:
            to = x.at[starts[i] : starts[i] + pieces[i].shape[0], :]
            rest_of_x.append(pltpu.make_async_copy(pieces[i], to, sems.at[i]))
    for copy in copies + rest_of_x:
        copy.start()
    for copy in copies:
        copy.wait()
    cells = Z * CELLS
    for at in (256, 768):
        rows = slice(at, at + CELLS)
        qkv[rows, :QKV] = nn(x[rows, :C], wq[...]).astype(BF16)
        qkv[rows, QKV:] = nt(x[rows, C:], wo[...]).astype(BF16)
    q = qkv[:, :PAIR] * jnp.bfloat16(0.125)
    k = qkv[:, PAIR : 2 * PAIR]
    v = qkv[:, 2 * PAIR : QKV]
    d = qkv[:, QKV:]
    zero = jnp.zeros_like(q)
    for head, mine_head in enumerate(heads()):
        qh = jnp.where(mine_head, q, zero)
        dh = jnp.where(mine_head, d, zero)
        scores = nt(qh, k)
        e = jnp.exp(scores - jnp.max(scores, -1, keepdims=True))
        p = e * (1.0 / jnp.sum(e, -1, keepdims=True))
        pb = p.astype(BF16)
        o = nn(pb, v).astype(BF16).astype(F32)
        delta = jnp.sum(dh.astype(F32) * o, -1, keepdims=True)
        ds = (p * (nt(dh, v) - delta)).astype(BF16)
        dq = (0.125 * nn(ds, k)).astype(BF16)
        dk, dv = tn(qh, ds), tn(dh, pb)
        if head == 0:
            att[...] = o.astype(BF16)
            dqkv[:, :PAIR] = dq
            turned[:PAIR, :] = dk
            turned[PAIR:, :] = dv
        else:
            att[...] = jnp.where(mine_head, o.astype(BF16), att[...])
            dqkv[:, :PAIR] = jnp.where(mine_head, dq, dqkv[:, :PAIR])
            turned[:PAIR, :] += dk
            turned[PAIR:, :] += dv

    dqkv[:, PAIR:] = turned[...].T.astype(BF16)
    for copy in rest_of_x:
        copy.wait()
    grad = tn(dqkv[...], x[:, :C]).T.astype(BF16)
    for lo in range(2):
        for xy in range(XY):
            at = (lo * XY + xy) * ROWS
            sent[xy, lo * ROWS : (lo + 1) * ROWS, :QKV] = grad[at : at + ROWS, :]
    grad = tn(att[...], x[:, C:]).astype(BF16)
    for xy in range(XY):
        col, y = divmod(xy, 4)
        for lo in range(2):
            at = (lo * 4 + col) * PAIR
            sent[xy, lo * ROWS : (lo + 1) * ROWS, QKV:] = grad[
                y * ROWS : (y + 1) * ROWS, at : at + PAIR
            ]
    copies = [pltpu.make_async_copy(sent, grads, sems.at[0])]
    copies[0].start()
    far, near = results[0], results[1]
    order = [(Z + 2, far)]
    order += [(Z + spot, near.at[i * CELLS : (i + 1) * CELLS]) for i, spot in enumerate((0, 1, 3))]
    order += list(zip((2, 0, 1, 3), results[2:]))
    for i, (spot, to) in enumerate(order):
        rows = slice(spot * CELLS, (spot + 1) * CELLS)
        terms[rows, :] = nt(dqkv[rows, :], wq[...]).astype(BF16)
        copies.append(pltpu.make_async_copy(terms.at[rows, :], to, sems.at[i + 1]))
        copies[-1].start()
    for copy in copies:
        copy.wait()


def attention(pieces, first, wq, wo):
    cells = 8 * CELLS
    return pl.pallas_call(
        attention_kernel,
        in_specs=[FAR] * (PIECES + 3),
        out_specs=[FAR] * 7,
        out_shape=(
            struct((XY, 2 * ROWS, QKV + PAIR)),
            struct((CELLS, C)),
            struct((3 * CELLS, C)),
            *[struct((CELLS, C))] * Z,
        ),
        scratch_shapes=[
            pltpu.VMEM((cells, 2 * C), BF16),
            pltpu.VMEM((C, QKV), BF16),
            pltpu.VMEM((PAIR, C), BF16),
            pltpu.VMEM((cells, QKV + PAIR), BF16),
            pltpu.VMEM((cells, PAIR), BF16),
            pltpu.VMEM((cells, QKV), BF16),
            pltpu.VMEM((2 * PAIR, cells), F32),
            pltpu.VMEM((XY, 2 * ROWS, QKV + PAIR), BF16),
            pltpu.VMEM((cells, C), BF16),
            pltpu.SemaphoreType.DMA((PIECES + 6,)),
        ],
        compiler_params=PARAMS,
        cost_estimate=pl.CostEstimate(
            flops=2**34, bytes_accessed=2**23, transcendentals=2 * cells * cells
        ),
    )(*pieces, first, wq, wo)


def normalize(image, row):
    xf = image.astype(F32)
    centered = xf - jnp.mean(xf, -1, keepdims=True)
    inverse = lax.rsqrt(jnp.mean(centered * centered, -1, keepdims=True) + 1e-05)
    return centered * inverse, inverse, 1.0 + row[:, :C].astype(F32)


def prepare_kernel(image, cot, row, x):
    xhat, _, scale = normalize(image[...], row[...])
    x[:, :C] = (xhat * scale + row[:, C:].astype(F32)).astype(BF16)
    x[:, C:] = cot[...]


def prepare(image, cot, row):
    return pl.pallas_call(
        prepare_kernel,
        in_specs=[WHOLE] * 3,
        out_shape=struct((CELLS, 2 * C)),
        cost_estimate=CHEAP,
        compiler_params=PARAMS,
    )(image, cot, row)


def cut_kernel(w_qkv, w_out, w_part, o_part, sems):
    space = lax.axis_index("space")
    copies = []
    for part in range(3):
        at = pl.multiple_of(part * C + space * PAIR, PAIR)
        to = w_part.at[:, part * PAIR : (part + 1) * PAIR]
        copies.append(pltpu.make_async_copy(w_qkv.at[:, pl.ds(at, PAIR)], to, sems.at[part]))
    for lo in range(2):
        at = pl.multiple_of(lo * 4 * PAIR + lax.rem(space, 4) * PAIR, PAIR)
        to = o_part.at[lo * ROWS : (lo + 1) * ROWS, :]
        copies.append(pltpu.make_async_copy(w_out.at[:, pl.ds(at, PAIR)], to, sems.at[3 + lo]))
    for copy in copies:
        copy.start()
    for copy in copies:
        copy.wait()


def cut(w_qkv, w_out):
    return pl.pallas_call(
        cut_kernel,
        in_specs=[FAR] * 2,
        out_shape=(struct((ROWS, QKV)), struct((2 * ROWS, PAIR))),
        scratch_shapes=[pltpu.SemaphoreType.DMA((5,))],
        cost_estimate=CHEAP,
        compiler_params=PARAMS,
    )(w_qkv, w_out)


def pack_kernel(where, w_part, w_far, o_part, packed):
    low = where[1] == 0
    near, far = w_part[...], w_far[...]
    packed[:ROWS, :QKV] = jnp.where(low, near, far)
    packed[ROWS:, :QKV] = jnp.where(low, far, near)
    packed[:, QKV:] = o_part[...]


def pack(where, w_part, w_far, o_part):
    return pl.pallas_call(
        pack_kernel,
        in_specs=[SCALARS] + [WHOLE] * 3,
        out_shape=struct((2 * ROWS, QKV + PAIR)),
        cost_estimate=CHEAP,
        compiler_params=SMALL,
    )(where, w_part, w_far, o_part)


def join_kernel(where, *refs):
    pieces, joined = refs[:-1], refs[-1]
    for far, piece in enumerate(pieces):
        joined[lax.rem(where[3] - far + 4, 4)] = piece[...]


def join(where, pieces):
    return pl.pallas_call(
        join_kernel,
        in_specs=[SCALARS] + [WHOLE] * 4,
        out_shape=struct((4, 2 * ROWS, QKV + PAIR)),
        cost_estimate=CHEAP,
        compiler_params=SMALL,
    )(where, *pieces)


def total_kernel(where, sent, near, far, go):
    total = sent[0].astype(F32)
    for xy in range(1, XY):
        total = total + sent[xy].astype(F32)
    go[...] = total[:, QKV:].astype(BF16)
    low = where[1] == 0
    first, second = total[:ROWS, :QKV], total[ROWS:, :QKV]
    near[...] = jnp.where(low, first, second)
    far[...] = jnp.where(low, second, first).astype(BF16)


def add_up(where, sent):
    return pl.pallas_call(
        total_kernel,
        in_specs=[SCALARS, WHOLE],
        out_shape=(struct((ROWS, QKV), F32), struct((ROWS, QKV)), struct((2 * ROWS, PAIR))),
        cost_estimate=CHEAP,
        compiler_params=SMALL,
    )(where, sent)


def finish_kernel(image, row, *refs):
    pieces, branch = refs[:-1], refs[-1]
    xhat, inverse, scale = normalize(image[...], row[...])
    dnormed = pieces[0][...].astype(F32)
    for piece in pieces[1:]:
        dnormed = dnormed + piece[...].astype(F32)
    dxhat = dnormed * scale
    mean = jnp.mean(dxhat, -1, keepdims=True)
    along = jnp.mean(dxhat * xhat, -1, keepdims=True)
    branch[...] = (inverse * (dxhat - mean - xhat * along)).astype(BF16)


def finish(image, row, pieces):
    return pl.pallas_call(
        finish_kernel,
        out_shape=struct((CELLS, C)),
        in_specs=[WHOLE] * (2 + len(pieces)),
        cost_estimate=CHEAP,
        compiler_params=SMALL,
    )(image, row, *pieces)


def place_kernel(where, *refs):
    pieces, (grad_q, grad_o) = refs[:-2], refs[-2:]
    z, core = where[0] // 2, lax.rem(where[0], 2)
    lane = lax.broadcasted_iota(jnp.int32, (1, 4 * PAIR), 1) // PAIR
    halves = [jnp.zeros((ROWS, 4 * PAIR), F32), jnp.zeros((ROWS, 4 * PAIR), F32)]
    for i, piece in enumerate(pieces):
        far, other = i % 4, i // 4
        place = lax.rem(z - far + Z, Z) * 2 + (core if other == 0 else 1 - core)
        for part in range(3):
            at = pl.multiple_of(part * C + place * PAIR, PAIR)
            grad_q[:, pl.ds(at, PAIR)] = piece[:, part * PAIR : (part + 1) * PAIR].astype(F32)
        mine = lane == lax.rem(place, 4)
        for lo in range(2):
            at = QKV + lo * PAIR
            value = piece[:, at : at + PAIR].astype(F32)
            halves[lo] = halves[lo] + jnp.where(mine, jnp.concatenate([value] * 4, 1), 0.0)
    grad_o[:, : 4 * PAIR] = halves[0]
    grad_o[:, 4 * PAIR :] = halves[1]


def place(pieces, where):
    return pl.pallas_call(
        place_kernel,
        in_specs=[SCALARS] + [WHOLE] * 8,
        out_shape=(struct((ROWS, 3 * C), F32), struct((ROWS, C), F32)),
        cost_estimate=CHEAP,
        compiler_params=SMALL,
    )(where, *pieces)


def turn(x, by):
    pairs = [(z * 2 + c, (z + by) % Z * 2 + c) for z in range(Z) for c in range(2)]
    return lax.ppermute(x, "space", pairs)


def swap(x):
    return lax.ppermute(x, "space", [(i, i ^ 1) for i in range(2 * Z)])


def swap_lo(x):
    return lax.ppermute(x, "dp", [(i, i ^ XY) for i in range(2 * XY)])


def transpose_devices(x):
    at = lambda t, y, s: (t * 4 + y) * 8 + s
    pairs = [(at(t, y, s), at(s, y, t)) for t in range(8) for y in range(4) for s in range(8)]
    return lax.ppermute(x, ("dp", "space"), pairs)


def turn_dp(x, by_x, by_y):
    at = lambda lo, col, y: (lo * 4 + col % 4) * 4 + y % 4
    pairs = [
        (at(lo, col, y), at(lo, col + by_x, y + by_y))
        for lo in range(2)
        for col in range(4)
        for y in range(4)
    ]
    return lax.ppermute(x, "dp", pairs)


def over_xy(x):
    groups = [list(range(XY)), list(range(XY, 2 * XY))]
    return lax.all_to_all(x, "dp", 0, 0, axis_index_groups=groups, tiled=True)


def add(a, b):
    return (a.astype(F32) + b.astype(F32)).astype(BF16)


def after(x, *others):
    return lax.optimization_barrier((x, others))[0]


def body(images, cotangent, w_qkv, w_out, film, timesteps):
    space, dp = lax.axis_index("space"), lax.axis_index("dp")
    where = jnp.stack([space, dp // XY, lax.rem(dp // 4, 4), lax.rem(dp, 4)])
    row = lax.dynamic_slice_in_dim(film, timesteps[0], 1, 0)
    image = images[0]
    w_part, o_part = cut(w_qkv, w_out)
    w_far, o_part = swap_lo(w_part), transpose_devices(o_part)
    x = prepare(image, cotangent[0], row)
    x = after(x, w_far, o_part)
    one, three = turn(x, 1), turn(x, 3)
    packed = pack(where, w_part, w_far, o_part)
    packed = [packed] + [turn_dp(packed, 0, by) for by in range(1, 4)]
    parts = join(where, packed)
    x = after(x, *packed)
    parts = [parts] + [turn_dp(parts, by, 0) for by in range(1, 4)]
    one, three = after((one, three), *parts)
    half = CELLS // 2
    two = turn(one[:half], 1), turn(three[half:], 3)
    others = [swap(piece) for piece in (x, one, three)]
    first, wq, wo = project(where, [x, one, three, *others], parts)
    two = after(two, first)
    pieces = [x, one, *two, three]
    pieces += [others[0], others[1], *[swap(piece) for piece in two], others[2]]
    grads, far, near, two, own, one, three = attention(pieces, first, wq, wo)
    grads = over_xy(grads)

    two = turn(add(two, swap(far)), 2)
    near = swap(near)
    own, one, three = (
        add(piece, near[i * CELLS : (i + 1) * CELLS]) for i, piece in enumerate((own, one, three))
    )
    one, three = turn(one, 3), turn(three, 1)
    branch = finish(image, row, (own, one, two, three))

    near, far, go = add_up(where, grads)
    go = transpose_devices(go)
    gq = (near + swap_lo(far).astype(F32)).astype(BF16)
    mine = jnp.concatenate([gq, go[:ROWS], go[ROWS:]], 1)
    mine = after(mine, two)
    every = [mine] + [turn(mine, by) for by in range(1, Z)]
    grad_q, grad_o = place(every + [swap(piece) for piece in every], where)
    return branch[None], grad_q, grad_o


def solution(mesh):
    return jax.shard_map(
        body,
        mesh=mesh,
        in_specs=(
            P("dp", "space", None),
            P("dp", "space", None),
            P("dp", None),
            P("dp", None),
            P(),
            P("dp"),
        ),
        out_specs=(P("dp", "space", None), P("dp", None), P("dp", None)),
        check_vma=False,
    )
```

```python
import jax
import jax.numpy as jnp
from jax import lax
from jax.experimental import pallas as pl
from jax.experimental.pallas import tpu as pltpu
from jax.sharding import PartitionSpec as P

C = 1024
Z = 4
XY = 16
ROWS = 32
CELLS = 128
PAIR = 128
QKV = 3 * PAIR
PIECES = 10
F32 = jnp.float32
BF16 = jnp.bfloat16
FAR = pl.BlockSpec(memory_space=pltpu.HBM)
WHOLE = pl.BlockSpec(memory_space=pltpu.VMEM)
SCALARS = pl.BlockSpec(memory_space=pltpu.SMEM)
CHEAP = pl.CostEstimate(flops=0, bytes_accessed=0, transcendentals=0)
SMALL = pltpu.CompilerParams(vmem_limit_bytes=8 * 2**20)
PARAMS = pltpu.CompilerParams(vmem_limit_bytes=58 * 2**20)


def nt(a, b):
    return lax.dot_general(a, b, (((1,), (1,)), ((), ())), preferred_element_type=F32)


def tn(a, b):
    return lax.dot_general(a, b, (((0,), (0,)), ((), ())), preferred_element_type=F32)


def nn(a, b):
    return jnp.dot(a, b, preferred_element_type=F32)


def struct(shape, dtype=BF16):
    return jax.ShapeDtypeStruct(shape, dtype)


def heads():
    lane = lax.broadcasted_iota(jnp.int32, (1, PAIR), 1)
    return lane < PAIR // 2, lane >= PAIR // 2


def project_kernel(where, *refs):
    pieces, parts, (qkvd, wq, wo, x) = refs[:6], refs[6:10], refs[10:]
    for far, part in enumerate(parts):
        col = lax.rem(where[2] - far + 4, 4)
        for lo in range(2):
            half = slice(lo * ROWS, (lo + 1) * ROWS)
            columns = pl.ds(pl.multiple_of((lo * 4 + col) * PAIR, PAIR), PAIR)
            for y in range(4):
                at = pl.multiple_of(((lo * 4 + col) * 4 + y) * ROWS, ROWS)
                wq[pl.ds(at, ROWS), :] = part[y, half, :QKV]
                wo[y * ROWS : (y + 1) * ROWS, columns] = part[y, half, QKV:]
    for i, piece in enumerate(pieces):
        x[i * CELLS : (i + 1) * CELLS, :] = piece[...]
    qkvd[:, :QKV] = nn(x[:, :C], wq[...]).astype(BF16)
    qkvd[:, QKV:] = nt(x[:, C:], wo[...]).astype(BF16)


def project(where, pieces, parts):
    return pl.pallas_call(
        project_kernel,
        in_specs=[SCALARS] + [WHOLE] * 10,
        out_shape=(struct((6 * CELLS, QKV + PAIR)), struct((C, QKV)), struct((PAIR, C))),
        scratch_shapes=[pltpu.VMEM((6 * CELLS, 2 * C), BF16)],
        compiler_params=PARAMS,
        cost_estimate=CHEAP,
    )(where, *pieces, *parts)


def attention_kernel(*refs):
    pieces, rest = refs[:PIECES], refs[PIECES:]
    first, wq_far, wo_far, grads, *results = rest[:10]
    x, wq, wo, qkv, att, dqkv, turned, sent, terms, sems = rest[10:]
    starts = (0, 128, 256, 320, 384, 512, 640, 768, 832, 896)
    late = (2, 3, 7, 8)
    copies = [pltpu.make_async_copy(wq_far, wq, sems.at[PIECES])]
    copies.append(pltpu.make_async_copy(wo_far, wo, sems.at[PIECES + 1]))
    for i in late:
        to = x.at[starts[i] : starts[i] + pieces[i].shape[0], :]
        copies.append(pltpu.make_async_copy(pieces[i], to, sems.at[i]))
    for i, (at, to, size) in enumerate(
        ((0, 0, 256), (256, 384, 128), (384, 512, 256), (640, 896, 128))
    ):
        source = first.at[at : at + size, :]
        copies.append(
            pltpu.make_async_copy(source, qkv.at[to : to + size, :], sems.at[PIECES + 2 + i])
        )
    rest_of_x = []
    for i in range(PIECES):
        if i not in late:
            to = x.at[starts[i] : starts[i] + pieces[i].shape[0], :]
            rest_of_x.append(pltpu.make_async_copy(pieces[i], to, sems.at[i]))
    for copy in copies + rest_of_x:
        copy.start()
    for copy in copies:
        copy.wait()
    cells = Z * CELLS
    for at in (256, 768):
        rows = slice(at, at + CELLS)
        qkv[rows, :QKV] = nn(x[rows, :C], wq[...]).astype(BF16)
        qkv[rows, QKV:] = nt(x[rows, C:], wo[...]).astype(BF16)
    q = qkv[:, :PAIR] * jnp.bfloat16(0.125)
    k = qkv[:, PAIR : 2 * PAIR]
    v = qkv[:, 2 * PAIR : QKV]
    d = qkv[:, QKV:]
    zero = jnp.zeros_like(q)
    for head, mine_head in enumerate(heads()):
        qh = jnp.where(mine_head, q, zero)
        dh = jnp.where(mine_head, d, zero)
        scores = nt(qh, k)
        e = jnp.exp(scores - jnp.max(scores, -1, keepdims=True))
        p = e * (1.0 / jnp.sum(e, -1, keepdims=True))
        pb = p.astype(BF16)
        o = nn(pb, v).astype(BF16).astype(F32)
        delta = jnp.sum(dh.astype(F32) * o, -1, keepdims=True)
        ds = (p * (nt(dh, v) - delta)).astype(BF16)
        dq = (0.125 * nn(ds, k)).astype(BF16)
        dk, dv = tn(qh, ds), tn(dh, pb)
        if head == 0:
            att[...] = o.astype(BF16)
            dqkv[:, :PAIR] = dq
            turned[:PAIR, :] = dk
            turned[PAIR:, :] = dv
        else:
            att[...] = jnp.where(mine_head, o.astype(BF16), att[...])
            dqkv[:, :PAIR] = jnp.where(mine_head, dq, dqkv[:, :PAIR])
            turned[:PAIR, :] += dk
            turned[PAIR:, :] += dv

    dqkv[:, PAIR:] = turned[...].T.astype(BF16)
    for copy in rest_of_x:
        copy.wait()
    grad = tn(dqkv[...], x[:, :C]).T.astype(BF16)
    for lo in range(2):
        for xy in range(XY):
            at = (lo * XY + xy) * ROWS
            sent[xy, lo * ROWS : (lo + 1) * ROWS, :QKV] = grad[at : at + ROWS, :]
    grad = tn(att[...], x[:, C:]).astype(BF16)
    for xy in range(XY):
        col, y = divmod(xy, 4)
        for lo in range(2):
            at = (lo * 4 + col) * PAIR
            sent[xy, lo * ROWS : (lo + 1) * ROWS, QKV:] = grad[
                y * ROWS : (y + 1) * ROWS, at : at + PAIR
            ]
    copies = [pltpu.make_async_copy(sent, grads, sems.at[0])]
    copies[0].start()
    far, near = results[0], results[1]
    order = [(Z + 2, far)]
    order += [(Z + spot, near.at[i * CELLS : (i + 1) * CELLS]) for i, spot in enumerate((0, 1, 3))]
    order += list(zip((2, 0, 1, 3), results[2:]))
    for i, (spot, to) in enumerate(order):
        rows = slice(spot * CELLS, (spot + 1) * CELLS)
        terms[rows, :] = nt(dqkv[rows, :], wq[...]).astype(BF16)
        copies.append(pltpu.make_async_copy(terms.at[rows, :], to, sems.at[i + 1]))
        copies[-1].start()
    for copy in copies:
        copy.wait()


def attention(pieces, first, wq, wo):
    cells = 8 * CELLS
    return pl.pallas_call(
        attention_kernel,
        in_specs=[FAR] * (PIECES + 3),
        out_specs=[FAR] * 7,
        out_shape=(
            struct((XY, 2 * ROWS, QKV + PAIR)),
            struct((CELLS, C)),
            struct((3 * CELLS, C)),
            *[struct((CELLS, C))] * Z,
        ),
        scratch_shapes=[
            pltpu.VMEM((cells, 2 * C), BF16),
            pltpu.VMEM((C, QKV), BF16),
            pltpu.VMEM((PAIR, C), BF16),
            pltpu.VMEM((cells, QKV + PAIR), BF16),
            pltpu.VMEM((cells, PAIR), BF16),
            pltpu.VMEM((cells, QKV), BF16),
            pltpu.VMEM((2 * PAIR, cells), F32),
            pltpu.VMEM((XY, 2 * ROWS, QKV + PAIR), BF16),
            pltpu.VMEM((cells, C), BF16),
            pltpu.SemaphoreType.DMA((PIECES + 6,)),
        ],
        compiler_params=PARAMS,
        cost_estimate=pl.CostEstimate(
            flops=2**34, bytes_accessed=2**23, transcendentals=2 * cells * cells
        ),
    )(*pieces, first, wq, wo)


def normalize(image, row):
    xf = image.astype(F32)
    centered = xf - jnp.mean(xf, -1, keepdims=True)
    inverse = lax.rsqrt(jnp.mean(centered * centered, -1, keepdims=True) + 1e-05)
    return centered * inverse, inverse, 1.0 + row[:, :C].astype(F32)


def prepare_kernel(image, cot, row, x):
    xhat, _, scale = normalize(image[...], row[...])
    x[:, :C] = (xhat * scale + row[:, C:].astype(F32)).astype(BF16)
    x[:, C:] = cot[...]


def prepare(image, cot, row):
    return pl.pallas_call(
        prepare_kernel,
        in_specs=[WHOLE] * 3,
        out_shape=struct((CELLS, 2 * C)),
        cost_estimate=CHEAP,
        compiler_params=PARAMS,
    )(image, cot, row)


def cut_kernel(w_qkv, w_out, w_part, o_part, sems):
    space = lax.axis_index("space")
    copies = []
    for part in range(3):
        at = pl.multiple_of(part * C + space * PAIR, PAIR)
        to = w_part.at[:, part * PAIR : (part + 1) * PAIR]
        copies.append(pltpu.make_async_copy(w_qkv.at[:, pl.ds(at, PAIR)], to, sems.at[part]))
    for lo in range(2):
        at = pl.multiple_of(lo * 4 * PAIR + lax.rem(space, 4) * PAIR, PAIR)
        to = o_part.at[lo * ROWS : (lo + 1) * ROWS, :]
        copies.append(pltpu.make_async_copy(w_out.at[:, pl.ds(at, PAIR)], to, sems.at[3 + lo]))
    for copy in copies:
        copy.start()
    for copy in copies:
        copy.wait()


def cut(w_qkv, w_out):
    return pl.pallas_call(
        cut_kernel,
        in_specs=[FAR] * 2,
        out_shape=(struct((ROWS, QKV)), struct((2 * ROWS, PAIR))),
        scratch_shapes=[pltpu.SemaphoreType.DMA((5,))],
        cost_estimate=CHEAP,
        compiler_params=PARAMS,
    )(w_qkv, w_out)


def pack_kernel(where, w_part, w_far, o_part, packed):
    low = where[1] == 0
    near, far = w_part[...], w_far[...]
    packed[:ROWS, :QKV] = jnp.where(low, near, far)
    packed[ROWS:, :QKV] = jnp.where(low, far, near)
    packed[:, QKV:] = o_part[...]


def pack(where, w_part, w_far, o_part):
    return pl.pallas_call(
        pack_kernel,
        in_specs=[SCALARS] + [WHOLE] * 3,
        out_shape=struct((2 * ROWS, QKV + PAIR)),
        cost_estimate=CHEAP,
        compiler_params=SMALL,
    )(where, w_part, w_far, o_part)


def join_kernel(where, *refs):
    pieces, joined = refs[:-1], refs[-1]
    for far, piece in enumerate(pieces):
        joined[lax.rem(where[3] - far + 4, 4)] = piece[...]


def join(where, pieces):
    return pl.pallas_call(
        join_kernel,
        in_specs=[SCALARS] + [WHOLE] * 4,
        out_shape=struct((4, 2 * ROWS, QKV + PAIR)),
        cost_estimate=CHEAP,
        compiler_params=SMALL,
    )(where, *pieces)


def total_kernel(where, sent, near, far, go):
    total = sent[0].astype(F32)
    for xy in range(1, XY):
        total = total + sent[xy].astype(F32)
    go[...] = total[:, QKV:].astype(BF16)
    low = where[1] == 0
    first, second = total[:ROWS, :QKV], total[ROWS:, :QKV]
    near[...] = jnp.where(low, first, second)
    far[...] = jnp.where(low, second, first).astype(BF16)


def add_up(where, sent):
    return pl.pallas_call(
        total_kernel,
        in_specs=[SCALARS, WHOLE],
        out_shape=(struct((ROWS, QKV), F32), struct((ROWS, QKV)), struct((2 * ROWS, PAIR))),
        cost_estimate=CHEAP,
        compiler_params=SMALL,
    )(where, sent)


def finish_kernel(image, row, *refs):
    pieces, branch = refs[:-1], refs[-1]
    xhat, inverse, scale = normalize(image[...], row[...])
    dnormed = pieces[0][...].astype(F32)
    for piece in pieces[1:]:
        dnormed = dnormed + piece[...].astype(F32)
    dxhat = dnormed * scale
    mean = jnp.mean(dxhat, -1, keepdims=True)
    along = jnp.mean(dxhat * xhat, -1, keepdims=True)
    branch[...] = (inverse * (dxhat - mean - xhat * along)).astype(BF16)


def finish(image, row, pieces):
    return pl.pallas_call(
        finish_kernel,
        out_shape=struct((CELLS, C)),
        in_specs=[WHOLE] * (2 + len(pieces)),
        cost_estimate=CHEAP,
        compiler_params=SMALL,
    )(image, row, *pieces)


def place_kernel(where, *refs):
    pieces, (grad_q, grad_o) = refs[:-2], refs[-2:]
    z, core = where[0] // 2, lax.rem(where[0], 2)
    lane = lax.broadcasted_iota(jnp.int32, (1, 4 * PAIR), 1) // PAIR
    halves = [jnp.zeros((ROWS, 4 * PAIR), F32), jnp.zeros((ROWS, 4 * PAIR), F32)]
    for i, piece in enumerate(pieces):
        far, other = i % 4, i // 4
        place = lax.rem(z - far + Z, Z) * 2 + (core if other == 0 else 1 - core)
        for part in range(3):
            at = pl.multiple_of(part * C + place * PAIR, PAIR)
            grad_q[:, pl.ds(at, PAIR)] = piece[:, part * PAIR : (part + 1) * PAIR].astype(F32)
        mine = lane == lax.rem(place, 4)
        for lo in range(2):
            at = QKV + lo * PAIR
            value = piece[:, at : at + PAIR].astype(F32)
            halves[lo] = halves[lo] + jnp.where(mine, jnp.concatenate([value] * 4, 1), 0.0)
    grad_o[:, : 4 * PAIR] = halves[0]
    grad_o[:, 4 * PAIR :] = halves[1]


def place(pieces, where):
    return pl.pallas_call(
        place_kernel,
        in_specs=[SCALARS] + [WHOLE] * 8,
        out_shape=(struct((ROWS, 3 * C), F32), struct((ROWS, C), F32)),
        cost_estimate=CHEAP,
        compiler_params=SMALL,
    )(where, *pieces)


def turn(x, by):
    pairs = [(z * 2 + c, (z + by) % Z * 2 + c) for z in range(Z) for c in range(2)]
    return lax.ppermute(x, "space", pairs)


def swap(x):
    return lax.ppermute(x, "space", [(i, i ^ 1) for i in range(2 * Z)])


def swap_lo(x):
    return lax.ppermute(x, "dp", [(i, i ^ XY) for i in range(2 * XY)])


def transpose_devices(x):
    at = lambda t, y, s: (t * 4 + y) * 8 + s
    pairs = [(at(t, y, s), at(s, y, t)) for t in range(8) for y in range(4) for s in range(8)]
    return lax.ppermute(x, ("dp", "space"), pairs)


def turn_dp(x, by_x, by_y):
    at = lambda lo, col, y: (lo * 4 + col % 4) * 4 + y % 4
    pairs = [
        (at(lo, col, y), at(lo, col + by_x, y + by_y))
        for lo in range(2)
        for col in range(4)
        for y in range(4)
    ]
    return lax.ppermute(x, "dp", pairs)


def over_xy(x):
    groups = [list(range(XY)), list(range(XY, 2 * XY))]
    return lax.all_to_all(x, "dp", 0, 0, axis_index_groups=groups, tiled=True)


def add(a, b):
    return (a.astype(F32) + b.astype(F32)).astype(BF16)


def after(x, *others):
    return lax.optimization_barrier((x, others))[0]


def body(images, cotangent, w_qkv, w_out, film, timesteps):
    space, dp = lax.axis_index("space"), lax.axis_index("dp")
    where = jnp.stack([space, dp // XY, lax.rem(dp // 4, 4), lax.rem(dp, 4)])
    row = lax.dynamic_slice_in_dim(film, timesteps[0], 1, 0)
    image = images[0]
    w_part, o_part = cut(w_qkv, w_out)
    w_far, o_part = swap_lo(w_part), transpose_devices(o_part)
    x = prepare(image, cotangent[0], row)
    x = after(x, w_far, o_part)
    one, three = turn(x, 1), turn(x, 3)
    packed = pack(where, w_part, w_far, o_part)
    packed = [packed] + [turn_dp(packed, 0, by) for by in range(1, 4)]
    parts = join(where, packed)
    x = after(x, *packed)
    parts = [parts] + [turn_dp(parts, by, 0) for by in range(1, 4)]
    one, three = after((one, three), *parts)
    half = CELLS // 2
    two = turn(one[:half], 1), turn(three[half:], 3)
    others = [swap(piece) for piece in (x, one, three)]
    first, wq, wo = project(where, [x, one, three, *others], parts)
    two = after(two, first)
    pieces = [x, one, *two, three]
    pieces += [others[0], others[1], *[swap(piece) for piece in two], others[2]]
    grads, far, near, two, own, one, three = attention(pieces, first, wq, wo)
    grads = over_xy(grads)

    two = turn(add(two, swap(far)), 2)
    near = swap(near)
    own, one, three = (
        add(piece, near[i * CELLS : (i + 1) * CELLS]) for i, piece in enumerate((own, one, three))
    )

    near, far, go = add_up(where, grads)
    go = transpose_devices(go)
    gq = (near + swap_lo(far).astype(F32)).astype(BF16)
    mine = jnp.concatenate([gq, go[:ROWS], go[ROWS:]], 1)
    mine = after(mine, two)
    one, three = turn(after(one, mine), 3), turn(after(three, mine), 1)
    every = [mine] + [turn(mine, by) for by in range(1, Z)]
    grad_q, grad_o = place(every + [swap(piece) for piece in every], where)
    branch = finish(image, row, (own, one, two, three))
    return branch[None], grad_q, grad_o


def solution(mesh):
    return jax.shard_map(
        body,
        mesh=mesh,
        in_specs=(
            P("dp", "space", None),
            P("dp", "space", None),
            P("dp", None),
            P("dp", None),
            P(),
            P("dp"),
        ),
        out_specs=(P("dp", "space", None), P("dp", None), P("dp", None)),
        check_vma=False,
    )
```

```python
import jax
import jax.numpy as jnp
from jax import lax
from jax.experimental import pallas as pl
from jax.experimental.pallas import tpu as pltpu
from jax.sharding import PartitionSpec as P

C = 1024
Z = 4
XY = 16
ROWS = 32
CELLS = 128
PAIR = 128
QKV = 3 * PAIR
PIECES = 10
F32 = jnp.float32
BF16 = jnp.bfloat16
FAR = pl.BlockSpec(memory_space=pltpu.HBM)
WHOLE = pl.BlockSpec(memory_space=pltpu.VMEM)
SCALARS = pl.BlockSpec(memory_space=pltpu.SMEM)
CHEAP = pl.CostEstimate(flops=0, bytes_accessed=0, transcendentals=0)
SMALL = pltpu.CompilerParams(vmem_limit_bytes=8 * 2**20)
PARAMS = pltpu.CompilerParams(vmem_limit_bytes=58 * 2**20)


def nt(a, b):
    return lax.dot_general(a, b, (((1,), (1,)), ((), ())), preferred_element_type=F32)


def tn(a, b):
    return lax.dot_general(a, b, (((0,), (0,)), ((), ())), preferred_element_type=F32)


def nn(a, b):
    return jnp.dot(a, b, preferred_element_type=F32)


def struct(shape, dtype=BF16):
    return jax.ShapeDtypeStruct(shape, dtype)


def heads():
    lane = lax.broadcasted_iota(jnp.int32, (1, PAIR), 1)
    return lane < PAIR // 2, lane >= PAIR // 2


def project_kernel(where, *refs):
    pieces, parts, (qkvd, wq, wo, x) = refs[:6], refs[6:10], refs[10:]
    for far, part in enumerate(parts):
        col = lax.rem(where[2] - far + 4, 4)
        for lo in range(2):
            half = slice(lo * ROWS, (lo + 1) * ROWS)
            columns = pl.ds(pl.multiple_of((lo * 4 + col) * PAIR, PAIR), PAIR)
            for y in range(4):
                at = pl.multiple_of(((lo * 4 + col) * 4 + y) * ROWS, ROWS)
                wq[pl.ds(at, ROWS), :] = part[y, half, :QKV]
                wo[y * ROWS : (y + 1) * ROWS, columns] = part[y, half, QKV:]
    for i, piece in enumerate(pieces):
        x[i * CELLS : (i + 1) * CELLS, :] = piece[...]
    qkvd[:, :QKV] = nn(x[:, :C], wq[...]).astype(BF16)
    qkvd[:, QKV:] = nt(x[:, C:], wo[...]).astype(BF16)


def project(where, pieces, parts):
    return pl.pallas_call(
        project_kernel,
        in_specs=[SCALARS] + [WHOLE] * 10,
        out_shape=(struct((6 * CELLS, QKV + PAIR)), struct((C, QKV)), struct((PAIR, C))),
        scratch_shapes=[pltpu.VMEM((6 * CELLS, 2 * C), BF16)],
        compiler_params=PARAMS,
        cost_estimate=CHEAP,
    )(where, *pieces, *parts)


def attention_kernel(*refs):
    pieces, rest = refs[:PIECES], refs[PIECES:]
    first, wq_far, wo_far, grads, *results = rest[:10]
    x, wq, wo, qkv, att, dqkv, turned, sent, terms, sems = rest[10:]
    starts = (0, 128, 256, 320, 384, 512, 640, 768, 832, 896)
    late = (2, 3, 7, 8)
    copies = [pltpu.make_async_copy(wq_far, wq, sems.at[PIECES])]
    copies.append(pltpu.make_async_copy(wo_far, wo, sems.at[PIECES + 1]))
    for i in late:
        to = x.at[starts[i] : starts[i] + pieces[i].shape[0], :]
        copies.append(pltpu.make_async_copy(pieces[i], to, sems.at[i]))
    for i, (at, to, size) in enumerate(
        ((0, 0, 256), (256, 384, 128), (384, 512, 256), (640, 896, 128))
    ):
        source = first.at[at : at + size, :]
        copies.append(
            pltpu.make_async_copy(source, qkv.at[to : to + size, :], sems.at[PIECES + 2 + i])
        )
    rest_of_x = []
    for i in range(PIECES):
        if i not in late:
            to = x.at[starts[i] : starts[i] + pieces[i].shape[0], :]
            rest_of_x.append(pltpu.make_async_copy(pieces[i], to, sems.at[i]))
    for copy in copies + rest_of_x:
        copy.start()
    for copy in copies:
        copy.wait()
    cells = Z * CELLS
    for at in (256, 768):
        rows = slice(at, at + CELLS)
        qkv[rows, :QKV] = nn(x[rows, :C], wq[...]).astype(BF16)
        qkv[rows, QKV:] = nt(x[rows, C:], wo[...]).astype(BF16)
    q = qkv[:, :PAIR] * jnp.bfloat16(0.125)
    k = qkv[:, PAIR : 2 * PAIR]
    v = qkv[:, 2 * PAIR : QKV]
    d = qkv[:, QKV:]
    zero = jnp.zeros_like(q)
    for head, mine_head in enumerate(heads()):
        qh = jnp.where(mine_head, q, zero)
        dh = jnp.where(mine_head, d, zero)
        scores = nt(qh, k)
        e = jnp.exp(scores - jnp.max(scores, -1, keepdims=True))
        p = e * (1.0 / jnp.sum(e, -1, keepdims=True))
        pb = p.astype(BF16)
        o = nn(pb, v).astype(BF16).astype(F32)
        delta = jnp.sum(dh.astype(F32) * o, -1, keepdims=True)
        ds = (p * (nt(dh, v) - delta)).astype(BF16)
        dq = (0.125 * nn(ds, k)).astype(BF16)
        dk, dv = tn(qh, ds), tn(dh, pb)
        if head == 0:
            att[...] = o.astype(BF16)
            dqkv[:, :PAIR] = dq
            turned[:PAIR, :] = dk
            turned[PAIR:, :] = dv
        else:
            att[...] = jnp.where(mine_head, o.astype(BF16), att[...])
            dqkv[:, :PAIR] = jnp.where(mine_head, dq, dqkv[:, :PAIR])
            turned[:PAIR, :] += dk
            turned[PAIR:, :] += dv

    dqkv[:, PAIR:] = turned[...].T.astype(BF16)
    for copy in rest_of_x:
        copy.wait()
    grad = tn(dqkv[...], x[:, :C]).T.astype(BF16)
    for lo in range(2):
        for xy in range(XY):
            at = (lo * XY + xy) * ROWS
            sent[xy, lo * ROWS : (lo + 1) * ROWS, :QKV] = grad[at : at + ROWS, :]
    grad = tn(att[...], x[:, C:]).astype(BF16)
    for xy in range(XY):
        col, y = divmod(xy, 4)
        for lo in range(2):
            at = (lo * 4 + col) * PAIR
            sent[xy, lo * ROWS : (lo + 1) * ROWS, QKV:] = grad[
                y * ROWS : (y + 1) * ROWS, at : at + PAIR
            ]
    copies = [pltpu.make_async_copy(sent, grads, sems.at[0])]
    copies[0].start()
    far, near = results[0], results[1]
    order = [(Z + 2, far)]
    order += [(Z + spot, near.at[i * CELLS : (i + 1) * CELLS]) for i, spot in enumerate((0, 1, 3))]
    order += list(zip((2, 0, 1, 3), results[2:]))
    for i, (spot, to) in enumerate(order):
        rows = slice(spot * CELLS, (spot + 1) * CELLS)
        terms[rows, :] = nt(dqkv[rows, :], wq[...]).astype(BF16)
        copies.append(pltpu.make_async_copy(terms.at[rows, :], to, sems.at[i + 1]))
        copies[-1].start()
    for copy in copies:
        copy.wait()


def attention(pieces, first, wq, wo):
    cells = 8 * CELLS
    return pl.pallas_call(
        attention_kernel,
        in_specs=[FAR] * (PIECES + 3),
        out_specs=[FAR] * 7,
        out_shape=(
            struct((XY, 2 * ROWS, QKV + PAIR)),
            struct((CELLS, C)),
            struct((3 * CELLS, C)),
            *[struct((CELLS, C))] * Z,
        ),
        scratch_shapes=[
            pltpu.VMEM((cells, 2 * C), BF16),
            pltpu.VMEM((C, QKV), BF16),
            pltpu.VMEM((PAIR, C), BF16),
            pltpu.VMEM((cells, QKV + PAIR), BF16),
            pltpu.VMEM((cells, PAIR), BF16),
            pltpu.VMEM((cells, QKV), BF16),
            pltpu.VMEM((2 * PAIR, cells), F32),
            pltpu.VMEM((XY, 2 * ROWS, QKV + PAIR), BF16),
            pltpu.VMEM((cells, C), BF16),
            pltpu.SemaphoreType.DMA((PIECES + 6,)),
        ],
        compiler_params=PARAMS,
        cost_estimate=pl.CostEstimate(
            flops=2**34, bytes_accessed=2**23, transcendentals=2 * cells * cells
        ),
    )(*pieces, first, wq, wo)


def normalize(image, row):
    xf = image.astype(F32)
    centered = xf - jnp.mean(xf, -1, keepdims=True)
    inverse = lax.rsqrt(jnp.mean(centered * centered, -1, keepdims=True) + 1e-05)
    return centered * inverse, inverse, 1.0 + row[:, :C].astype(F32)


def prepare_kernel(image, cot, row, x):
    xhat, _, scale = normalize(image[...], row[...])
    x[:, :C] = (xhat * scale + row[:, C:].astype(F32)).astype(BF16)
    x[:, C:] = cot[...]


def prepare(image, cot, row):
    return pl.pallas_call(
        prepare_kernel,
        in_specs=[WHOLE] * 3,
        out_shape=struct((CELLS, 2 * C)),
        cost_estimate=CHEAP,
        compiler_params=PARAMS,
    )(image, cot, row)


def cut_kernel(w_qkv, w_out, w_part, o_part, sems):
    space = lax.axis_index("space")
    copies = []
    for part in range(3):
        at = pl.multiple_of(part * C + space * PAIR, PAIR)
        to = w_part.at[:, part * PAIR : (part + 1) * PAIR]
        copies.append(pltpu.make_async_copy(w_qkv.at[:, pl.ds(at, PAIR)], to, sems.at[part]))
    for lo in range(2):
        at = pl.multiple_of(lo * 4 * PAIR + lax.rem(space, 4) * PAIR, PAIR)
        to = o_part.at[lo * ROWS : (lo + 1) * ROWS, :]
        copies.append(pltpu.make_async_copy(w_out.at[:, pl.ds(at, PAIR)], to, sems.at[3 + lo]))
    for copy in copies:
        copy.start()
    for copy in copies:
        copy.wait()


def cut(w_qkv, w_out):
    return pl.pallas_call(
        cut_kernel,
        in_specs=[FAR] * 2,
        out_shape=(struct((ROWS, QKV)), struct((2 * ROWS, PAIR))),
        scratch_shapes=[pltpu.SemaphoreType.DMA((5,))],
        cost_estimate=CHEAP,
        compiler_params=PARAMS,
    )(w_qkv, w_out)


def pack_kernel(where, w_part, w_far, o_part, packed):
    low = where[1] == 0
    near, far = w_part[...], w_far[...]
    packed[:ROWS, :QKV] = jnp.where(low, near, far)
    packed[ROWS:, :QKV] = jnp.where(low, far, near)
    packed[:, QKV:] = o_part[...]


def pack(where, w_part, w_far, o_part):
    return pl.pallas_call(
        pack_kernel,
        in_specs=[SCALARS] + [WHOLE] * 3,
        out_shape=struct((2 * ROWS, QKV + PAIR)),
        cost_estimate=CHEAP,
        compiler_params=SMALL,
    )(where, w_part, w_far, o_part)


def join_kernel(where, *refs):
    pieces, joined = refs[:-1], refs[-1]
    for far, piece in enumerate(pieces):
        joined[lax.rem(where[3] - far + 4, 4)] = piece[...]


def join(where, pieces):
    return pl.pallas_call(
        join_kernel,
        in_specs=[SCALARS] + [WHOLE] * 4,
        out_shape=struct((4, 2 * ROWS, QKV + PAIR)),
        cost_estimate=CHEAP,
        compiler_params=SMALL,
    )(where, *pieces)


def total_kernel(where, sent, near, far, go):
    total = sent[0].astype(F32)
    for xy in range(1, XY):
        total = total + sent[xy].astype(F32)
    go[...] = total[:, QKV:].astype(BF16)
    low = where[1] == 0
    first, second = total[:ROWS, :QKV], total[ROWS:, :QKV]
    near[...] = jnp.where(low, first, second)
    far[...] = jnp.where(low, second, first).astype(BF16)


def add_up(where, sent):
    return pl.pallas_call(
        total_kernel,
        in_specs=[SCALARS, WHOLE],
        out_shape=(struct((ROWS, QKV), F32), struct((ROWS, QKV)), struct((2 * ROWS, PAIR))),
        cost_estimate=CHEAP,
        compiler_params=SMALL,
    )(where, sent)


def finish_kernel(image, row, *refs):
    pieces, branch = refs[:-1], refs[-1]
    xhat, inverse, scale = normalize(image[...], row[...])
    dnormed = pieces[0][...].astype(F32)
    for piece in pieces[1:]:
        dnormed = dnormed + piece[...].astype(F32)
    dxhat = dnormed * scale
    mean = jnp.mean(dxhat, -1, keepdims=True)
    along = jnp.mean(dxhat * xhat, -1, keepdims=True)
    branch[...] = (inverse * (dxhat - mean - xhat * along)).astype(BF16)


def finish(image, row, pieces):
    return pl.pallas_call(
        finish_kernel,
        out_shape=struct((CELLS, C)),
        in_specs=[WHOLE] * (2 + len(pieces)),
        cost_estimate=CHEAP,
        compiler_params=SMALL,
    )(image, row, *pieces)


def place_kernel(where, *refs):
    pieces, (grad_q, grad_o) = refs[:-2], refs[-2:]
    z, core = where[0] // 2, lax.rem(where[0], 2)
    lane = lax.broadcasted_iota(jnp.int32, (1, 4 * PAIR), 1) // PAIR
    halves = [jnp.zeros((ROWS, 4 * PAIR), F32), jnp.zeros((ROWS, 4 * PAIR), F32)]
    for i, piece in enumerate(pieces):
        far, other = i % 4, i // 4
        place = lax.rem(z - far + Z, Z) * 2 + (core if other == 0 else 1 - core)
        for part in range(3):
            at = pl.multiple_of(part * C + place * PAIR, PAIR)
            grad_q[:, pl.ds(at, PAIR)] = piece[:, part * PAIR : (part + 1) * PAIR].astype(F32)
        mine = lane == lax.rem(place, 4)
        for lo in range(2):
            at = QKV + lo * PAIR
            value = piece[:, at : at + PAIR].astype(F32)
            halves[lo] = halves[lo] + jnp.where(mine, jnp.concatenate([value] * 4, 1), 0.0)
    grad_o[:, : 4 * PAIR] = halves[0]
    grad_o[:, 4 * PAIR :] = halves[1]


def place(pieces, where):
    return pl.pallas_call(
        place_kernel,
        in_specs=[SCALARS] + [WHOLE] * 8,
        out_shape=(struct((ROWS, 3 * C), F32), struct((ROWS, C), F32)),
        cost_estimate=CHEAP,
        compiler_params=SMALL,
    )(where, *pieces)


def turn(x, by):
    pairs = [(z * 2 + c, (z + by) % Z * 2 + c) for z in range(Z) for c in range(2)]
    return lax.ppermute(x, "space", pairs)


def swap(x):
    return lax.ppermute(x, "space", [(i, i ^ 1) for i in range(2 * Z)])


def swap_lo(x):
    return lax.ppermute(x, "dp", [(i, i ^ XY) for i in range(2 * XY)])


def transpose_devices(x):
    at = lambda t, y, s: (t * 4 + y) * 8 + s
    pairs = [(at(t, y, s), at(s, y, t)) for t in range(8) for y in range(4) for s in range(8)]
    return lax.ppermute(x, ("dp", "space"), pairs)


def turn_dp(x, by_x, by_y):
    at = lambda lo, col, y: (lo * 4 + col % 4) * 4 + y % 4
    pairs = [
        (at(lo, col, y), at(lo, col + by_x, y + by_y))
        for lo in range(2)
        for col in range(4)
        for y in range(4)
    ]
    return lax.ppermute(x, "dp", pairs)


def over_xy(x):
    groups = [list(range(XY)), list(range(XY, 2 * XY))]
    return lax.all_to_all(x, "dp", 0, 0, axis_index_groups=groups, tiled=True)


def add(a, b):
    return (a.astype(F32) + b.astype(F32)).astype(BF16)


def after(x, *others):
    return lax.optimization_barrier((x, others))[0]


def body(images, cotangent, w_qkv, w_out, film, timesteps):
    space, dp = lax.axis_index("space"), lax.axis_index("dp")
    where = jnp.stack([space, dp // XY, lax.rem(dp // 4, 4), lax.rem(dp, 4)])
    row = lax.dynamic_slice_in_dim(film, timesteps[0], 1, 0)
    image = images[0]
    w_part, o_part = cut(w_qkv, w_out)
    w_far, o_part = swap_lo(w_part), transpose_devices(o_part)
    x = prepare(image, cotangent[0], row)
    x = after(x, w_far, o_part)
    one, three = turn(x, 1), turn(x, 3)
    packed = pack(where, w_part, w_far, o_part)
    packed = [packed] + [turn_dp(packed, 0, by) for by in range(1, 4)]
    parts = join(where, packed)
    x = after(x, *packed)
    parts = [parts] + [turn_dp(parts, by, 0) for by in range(1, 4)]
    one, three = after((one, three), *parts)
    half = CELLS // 2
    two = turn(one[:half], 1), turn(three[half:], 3)
    others = [swap(piece) for piece in (x, one, three)]
    first, wq, wo = project(where, [x, one, three, *others], parts)
    two = after(two, first)
    pieces = [x, one, *two, three]
    pieces += [others[0], others[1], *[swap(piece) for piece in two], others[2]]
    grads, far, near, two, own, one, three = attention(pieces, first, wq, wo)
    grads = over_xy(grads)

    two = turn(add(two, swap(far)), 2)
    near = swap(near)
    own, one, three = (
        add(piece, near[i * CELLS : (i + 1) * CELLS]) for i, piece in enumerate((own, one, three))
    )

    near, far, go = add_up(where, grads)
    go = transpose_devices(go)
    gq = (near + swap_lo(far).astype(F32)).astype(BF16)
    mine = jnp.concatenate([gq, go[:ROWS], go[ROWS:]], 1)
    mine = after(mine, two)
    one, three = turn(after(one, mine), 3), turn(after(three, mine), 1)
    every = [mine] + [turn(mine, by) for by in range(1, Z)]
    branch = finish(image, row, (own, one, two, three))
    every += [swap(piece) for piece in every]
    grad_q, grad_o = place([after(mine, branch), *every[1:]], where)
    return branch[None], grad_q, grad_o


def solution(mesh):
    return jax.shard_map(
        body,
        mesh=mesh,
        in_specs=(
            P("dp", "space", None),
            P("dp", "space", None),
            P("dp", None),
            P("dp", None),
            P(),
            P("dp"),
        ),
        out_specs=(P("dp", "space", None), P("dp", None), P("dp", None)),
        check_vma=False,
    )
```

```python
import jax
import jax.numpy as jnp
from jax import lax
from jax.experimental import pallas as pl
from jax.experimental.pallas import tpu as pltpu
from jax.sharding import PartitionSpec as P

C = 1024
Z = 4
XY = 16
ROWS = 32
CELLS = 128
PAIR = 128
QKV = 3 * PAIR
PIECES = 10
F32 = jnp.float32
BF16 = jnp.bfloat16
FAR = pl.BlockSpec(memory_space=pltpu.HBM)
WHOLE = pl.BlockSpec(memory_space=pltpu.VMEM)
SCALARS = pl.BlockSpec(memory_space=pltpu.SMEM)
CHEAP = pl.CostEstimate(flops=0, bytes_accessed=0, transcendentals=0)
SMALL = pltpu.CompilerParams(vmem_limit_bytes=8 * 2**20)
PARAMS = pltpu.CompilerParams(vmem_limit_bytes=58 * 2**20)


def nt(a, b):
    return lax.dot_general(a, b, (((1,), (1,)), ((), ())), preferred_element_type=F32)


def tn(a, b):
    return lax.dot_general(a, b, (((0,), (0,)), ((), ())), preferred_element_type=F32)


def nn(a, b):
    return jnp.dot(a, b, preferred_element_type=F32)


def struct(shape, dtype=BF16):
    return jax.ShapeDtypeStruct(shape, dtype)


def heads():
    lane = lax.broadcasted_iota(jnp.int32, (1, PAIR), 1)
    return lane < PAIR // 2, lane >= PAIR // 2


def project_kernel(where, *refs):
    pieces, parts, (qkvd, wq, wo, x) = refs[:6], refs[6:10], refs[10:]
    for far, part in enumerate(parts):
        col = lax.rem(where[2] - far + 4, 4)
        for lo in range(2):
            half = slice(lo * ROWS, (lo + 1) * ROWS)
            columns = pl.ds(pl.multiple_of((lo * 4 + col) * PAIR, PAIR), PAIR)
            for y in range(4):
                at = pl.multiple_of(((lo * 4 + col) * 4 + y) * ROWS, ROWS)
                wq[pl.ds(at, ROWS), :] = part[y, half, :QKV]
                wo[y * ROWS : (y + 1) * ROWS, columns] = part[y, half, QKV:]
    for i, piece in enumerate(pieces):
        x[i * CELLS : (i + 1) * CELLS, :] = piece[...]
    qkvd[:, :QKV] = nn(x[:, :C], wq[...]).astype(BF16)
    qkvd[:, QKV:] = nt(x[:, C:], wo[...]).astype(BF16)


def project(where, pieces, parts):
    return pl.pallas_call(
        project_kernel,
        in_specs=[SCALARS] + [WHOLE] * 10,
        out_shape=(struct((6 * CELLS, QKV + PAIR)), struct((C, QKV)), struct((PAIR, C))),
        scratch_shapes=[pltpu.VMEM((6 * CELLS, 2 * C), BF16)],
        compiler_params=PARAMS,
        cost_estimate=CHEAP,
    )(where, *pieces, *parts)


def attention_kernel(*refs):
    pieces, rest = refs[:PIECES], refs[PIECES:]
    first, wq_far, wo_far, grads, dqkv_far = rest[:5]
    x, wq, wo, qkv, att, dqkv, turned, sent, sems = rest[5:]
    starts = (0, 128, 256, 320, 384, 512, 640, 768, 832, 896)
    late = (2, 3, 7, 8)
    copies = [pltpu.make_async_copy(wq_far, wq, sems.at[PIECES])]
    copies.append(pltpu.make_async_copy(wo_far, wo, sems.at[PIECES + 1]))
    for i in late:
        to = x.at[starts[i] : starts[i] + pieces[i].shape[0], :]
        copies.append(pltpu.make_async_copy(pieces[i], to, sems.at[i]))
    for i, (at, to, size) in enumerate(
        ((0, 0, 256), (256, 384, 128), (384, 512, 256), (640, 896, 128))
    ):
        source = first.at[at : at + size, :]
        copies.append(
            pltpu.make_async_copy(source, qkv.at[to : to + size, :], sems.at[PIECES + 2 + i])
        )
    rest_of_x = []
    for i in range(PIECES):
        if i not in late:
            to = x.at[starts[i] : starts[i] + pieces[i].shape[0], :]
            rest_of_x.append(pltpu.make_async_copy(pieces[i], to, sems.at[i]))
    for copy in copies + rest_of_x:
        copy.start()
    for copy in copies:
        copy.wait()
    cells = Z * CELLS
    for at in (256, 768):
        rows = slice(at, at + CELLS)
        qkv[rows, :QKV] = nn(x[rows, :C], wq[...]).astype(BF16)
        qkv[rows, QKV:] = nt(x[rows, C:], wo[...]).astype(BF16)
    q = qkv[:, :PAIR] * jnp.bfloat16(0.125)
    k = qkv[:, PAIR : 2 * PAIR]
    v = qkv[:, 2 * PAIR : QKV]
    d = qkv[:, QKV:]
    zero = jnp.zeros_like(q)
    for head, mine_head in enumerate(heads()):
        qh = jnp.where(mine_head, q, zero)
        dh = jnp.where(mine_head, d, zero)
        scores = nt(qh, k)
        e = jnp.exp(scores - jnp.max(scores, -1, keepdims=True))
        p = e * (1.0 / jnp.sum(e, -1, keepdims=True))
        pb = p.astype(BF16)
        o = nn(pb, v).astype(BF16).astype(F32)
        delta = jnp.sum(dh.astype(F32) * o, -1, keepdims=True)
        ds = (p * (nt(dh, v) - delta)).astype(BF16)
        dq = (0.125 * nn(ds, k)).astype(BF16)
        dk, dv = tn(qh, ds), tn(dh, pb)
        if head == 0:
            att[...] = o.astype(BF16)
            dqkv[:, :PAIR] = dq
            turned[:PAIR, :] = dk
            turned[PAIR:, :] = dv
        else:
            att[...] = jnp.where(mine_head, o.astype(BF16), att[...])
            dqkv[:, :PAIR] = jnp.where(mine_head, dq, dqkv[:, :PAIR])
            turned[:PAIR, :] += dk
            turned[PAIR:, :] += dv

    dqkv[:, PAIR:] = turned[...].T.astype(BF16)
    early = pltpu.make_async_copy(dqkv, dqkv_far, sems.at[PIECES])
    early.start()
    for copy in rest_of_x:
        copy.wait()
    grad = tn(dqkv[...], x[:, :C]).T.astype(BF16)
    for lo in range(2):
        for xy in range(XY):
            at = (lo * XY + xy) * ROWS
            sent[xy, lo * ROWS : (lo + 1) * ROWS, :QKV] = grad[at : at + ROWS, :]
    grad = tn(att[...], x[:, C:]).astype(BF16)
    for xy in range(XY):
        col, y = divmod(xy, 4)
        for lo in range(2):
            at = (lo * 4 + col) * PAIR
            sent[xy, lo * ROWS : (lo + 1) * ROWS, QKV:] = grad[
                y * ROWS : (y + 1) * ROWS, at : at + PAIR
            ]
    copy = pltpu.make_async_copy(sent, grads, sems.at[0])
    copy.start()
    copy.wait()
    early.wait()


def terms_kernel(dqkv, wq, far, near, two, own, one, three):
    order = [(Z + 2, far)]
    order += [(Z + spot, near.at[i * CELLS : (i + 1) * CELLS]) for i, spot in enumerate((0, 1, 3))]
    order += [(2, two), (0, own), (1, one), (3, three)]
    for spot, to in order:
        rows = slice(spot * CELLS, (spot + 1) * CELLS)
        to[...] = nt(dqkv[rows, :], wq[...]).astype(BF16)


def dnormed_terms(dqkv, wq):
    return pl.pallas_call(
        terms_kernel,
        out_shape=(
            struct((CELLS, C)),
            struct((3 * CELLS, C)),
            *[struct((CELLS, C))] * Z,
        ),
        compiler_params=pltpu.CompilerParams(vmem_limit_bytes=16 * 2**20),
        cost_estimate=pl.CostEstimate(flops=2**34, bytes_accessed=2**23, transcendentals=0),
    )(dqkv, wq)


def attention(pieces, first, wq, wo):
    cells = 8 * CELLS
    return pl.pallas_call(
        attention_kernel,
        in_specs=[FAR] * (PIECES + 3),
        out_specs=[FAR] * 2,
        out_shape=(struct((XY, 2 * ROWS, QKV + PAIR)), struct((cells, QKV))),
        scratch_shapes=[
            pltpu.VMEM((cells, 2 * C), BF16),
            pltpu.VMEM((C, QKV), BF16),
            pltpu.VMEM((PAIR, C), BF16),
            pltpu.VMEM((cells, QKV + PAIR), BF16),
            pltpu.VMEM((cells, PAIR), BF16),
            pltpu.VMEM((cells, QKV), BF16),
            pltpu.VMEM((2 * PAIR, cells), F32),
            pltpu.VMEM((XY, 2 * ROWS, QKV + PAIR), BF16),
            pltpu.SemaphoreType.DMA((PIECES + 6,)),
        ],
        compiler_params=PARAMS,
        cost_estimate=pl.CostEstimate(
            flops=2**34, bytes_accessed=2**23, transcendentals=2 * cells * cells
        ),
    )(*pieces, first, wq, wo)


def normalize(image, row):
    xf = image.astype(F32)
    centered = xf - jnp.mean(xf, -1, keepdims=True)
    inverse = lax.rsqrt(jnp.mean(centered * centered, -1, keepdims=True) + 1e-05)
    return centered * inverse, inverse, 1.0 + row[:, :C].astype(F32)


def prepare_kernel(image, cot, row, x):
    xhat, _, scale = normalize(image[...], row[...])
    x[:, :C] = (xhat * scale + row[:, C:].astype(F32)).astype(BF16)
    x[:, C:] = cot[...]


def prepare(image, cot, row):
    return pl.pallas_call(
        prepare_kernel,
        in_specs=[WHOLE] * 3,
        out_shape=struct((CELLS, 2 * C)),
        cost_estimate=CHEAP,
        compiler_params=PARAMS,
    )(image, cot, row)


def cut_kernel(w_qkv, w_out, w_part, o_part, sems):
    space = lax.axis_index("space")
    copies = []
    for part in range(3):
        at = pl.multiple_of(part * C + space * PAIR, PAIR)
        to = w_part.at[:, part * PAIR : (part + 1) * PAIR]
        copies.append(pltpu.make_async_copy(w_qkv.at[:, pl.ds(at, PAIR)], to, sems.at[part]))
    for lo in range(2):
        at = pl.multiple_of(lo * 4 * PAIR + lax.rem(space, 4) * PAIR, PAIR)
        to = o_part.at[lo * ROWS : (lo + 1) * ROWS, :]
        copies.append(pltpu.make_async_copy(w_out.at[:, pl.ds(at, PAIR)], to, sems.at[3 + lo]))
    for copy in copies:
        copy.start()
    for copy in copies:
        copy.wait()


def cut(w_qkv, w_out):
    return pl.pallas_call(
        cut_kernel,
        in_specs=[FAR] * 2,
        out_shape=(struct((ROWS, QKV)), struct((2 * ROWS, PAIR))),
        scratch_shapes=[pltpu.SemaphoreType.DMA((5,))],
        cost_estimate=CHEAP,
        compiler_params=PARAMS,
    )(w_qkv, w_out)


def pack_kernel(where, w_part, w_far, o_part, packed):
    low = where[1] == 0
    near, far = w_part[...], w_far[...]
    packed[:ROWS, :QKV] = jnp.where(low, near, far)
    packed[ROWS:, :QKV] = jnp.where(low, far, near)
    packed[:, QKV:] = o_part[...]


def pack(where, w_part, w_far, o_part):
    return pl.pallas_call(
        pack_kernel,
        in_specs=[SCALARS] + [WHOLE] * 3,
        out_shape=struct((2 * ROWS, QKV + PAIR)),
        cost_estimate=CHEAP,
        compiler_params=SMALL,
    )(where, w_part, w_far, o_part)


def join_kernel(where, *refs):
    pieces, joined = refs[:-1], refs[-1]
    for far, piece in enumerate(pieces):
        joined[lax.rem(where[3] - far + 4, 4)] = piece[...]


def join(where, pieces):
    return pl.pallas_call(
        join_kernel,
        in_specs=[SCALARS] + [WHOLE] * 4,
        out_shape=struct((4, 2 * ROWS, QKV + PAIR)),
        cost_estimate=CHEAP,
        compiler_params=SMALL,
    )(where, *pieces)


def total_kernel(where, sent, near, far, go):
    total = sent[0].astype(F32)
    for xy in range(1, XY):
        total = total + sent[xy].astype(F32)
    go[...] = total[:, QKV:].astype(BF16)
    low = where[1] == 0
    first, second = total[:ROWS, :QKV], total[ROWS:, :QKV]
    near[...] = jnp.where(low, first, second)
    far[...] = jnp.where(low, second, first).astype(BF16)


def add_up(where, sent):
    return pl.pallas_call(
        total_kernel,
        in_specs=[SCALARS, WHOLE],
        out_shape=(struct((ROWS, QKV), F32), struct((ROWS, QKV)), struct((2 * ROWS, PAIR))),
        cost_estimate=CHEAP,
        compiler_params=SMALL,
    )(where, sent)


def finish_kernel(image, row, *refs):
    pieces, branch = refs[:-1], refs[-1]
    xhat, inverse, scale = normalize(image[...], row[...])
    dnormed = pieces[0][...].astype(F32)
    for piece in pieces[1:]:
        dnormed = dnormed + piece[...].astype(F32)
    dxhat = dnormed * scale
    mean = jnp.mean(dxhat, -1, keepdims=True)
    along = jnp.mean(dxhat * xhat, -1, keepdims=True)
    branch[...] = (inverse * (dxhat - mean - xhat * along)).astype(BF16)


def finish(image, row, pieces):
    return pl.pallas_call(
        finish_kernel,
        out_shape=struct((CELLS, C)),
        in_specs=[WHOLE] * (2 + len(pieces)),
        cost_estimate=CHEAP,
        compiler_params=SMALL,
    )(image, row, *pieces)


def place_kernel(where, *refs):
    pieces, (grad_q, grad_o) = refs[:-2], refs[-2:]
    z, core = where[0] // 2, lax.rem(where[0], 2)
    lane = lax.broadcasted_iota(jnp.int32, (1, 4 * PAIR), 1) // PAIR
    halves = [jnp.zeros((ROWS, 4 * PAIR), F32), jnp.zeros((ROWS, 4 * PAIR), F32)]
    for i, piece in enumerate(pieces):
        far, other = i % 4, i // 4
        place = lax.rem(z - far + Z, Z) * 2 + (core if other == 0 else 1 - core)
        for part in range(3):
            at = pl.multiple_of(part * C + place * PAIR, PAIR)
            grad_q[:, pl.ds(at, PAIR)] = piece[:, part * PAIR : (part + 1) * PAIR].astype(F32)
        mine = lane == lax.rem(place, 4)
        for lo in range(2):
            at = QKV + lo * PAIR
            value = piece[:, at : at + PAIR].astype(F32)
            halves[lo] = halves[lo] + jnp.where(mine, jnp.concatenate([value] * 4, 1), 0.0)
    grad_o[:, : 4 * PAIR] = halves[0]
    grad_o[:, 4 * PAIR :] = halves[1]


def place(pieces, where):
    return pl.pallas_call(
        place_kernel,
        in_specs=[SCALARS] + [WHOLE] * 8,
        out_shape=(struct((ROWS, 3 * C), F32), struct((ROWS, C), F32)),
        cost_estimate=CHEAP,
        compiler_params=SMALL,
    )(where, *pieces)


def turn(x, by):
    pairs = [(z * 2 + c, (z + by) % Z * 2 + c) for z in range(Z) for c in range(2)]
    return lax.ppermute(x, "space", pairs)


def swap(x):
    return lax.ppermute(x, "space", [(i, i ^ 1) for i in range(2 * Z)])


def swap_lo(x):
    return lax.ppermute(x, "dp", [(i, i ^ XY) for i in range(2 * XY)])


def transpose_devices(x):
    at = lambda t, y, s: (t * 4 + y) * 8 + s
    pairs = [(at(t, y, s), at(s, y, t)) for t in range(8) for y in range(4) for s in range(8)]
    return lax.ppermute(x, ("dp", "space"), pairs)


def turn_dp(x, by_x, by_y):
    at = lambda lo, col, y: (lo * 4 + col % 4) * 4 + y % 4
    pairs = [
        (at(lo, col, y), at(lo, col + by_x, y + by_y))
        for lo in range(2)
        for col in range(4)
        for y in range(4)
    ]
    return lax.ppermute(x, "dp", pairs)


def over_xy(x):
    groups = [list(range(XY)), list(range(XY, 2 * XY))]
    return lax.all_to_all(x, "dp", 0, 0, axis_index_groups=groups, tiled=True)


def add(a, b):
    return (a.astype(F32) + b.astype(F32)).astype(BF16)


def after(x, *others):
    return lax.optimization_barrier((x, others))[0]


def body(images, cotangent, w_qkv, w_out, film, timesteps):
    space, dp = lax.axis_index("space"), lax.axis_index("dp")
    where = jnp.stack([space, dp // XY, lax.rem(dp // 4, 4), lax.rem(dp, 4)])
    row = lax.dynamic_slice_in_dim(film, timesteps[0], 1, 0)
    image = images[0]
    w_part, o_part = cut(w_qkv, w_out)
    w_far, o_part = swap_lo(w_part), transpose_devices(o_part)
    x = prepare(image, cotangent[0], row)
    x = after(x, w_far, o_part)
    one, three = turn(x, 1), turn(x, 3)
    packed = pack(where, w_part, w_far, o_part)
    packed = [packed] + [turn_dp(packed, 0, by) for by in range(1, 4)]
    parts = join(where, packed)
    x = after(x, *packed)
    parts = [parts] + [turn_dp(parts, by, 0) for by in range(1, 4)]
    one, three = after((one, three), *parts)
    half = CELLS // 2
    two = turn(one[:half], 1), turn(three[half:], 3)
    others = [swap(piece) for piece in (x, one, three)]
    first, wq, wo = project(where, [x, one, three, *others], parts)
    two = after(two, first)
    pieces = [x, one, *two, three]
    pieces += [others[0], others[1], *[swap(piece) for piece in two], others[2]]
    grads, dqkv = attention(pieces, first, wq, wo)
    grads = over_xy(grads)
    far, near, two, own, one, three = dnormed_terms(dqkv, wq)

    two = turn(add(two, swap(far)), 2)
    near = swap(near)
    own, one, three = (
        add(piece, near[i * CELLS : (i + 1) * CELLS]) for i, piece in enumerate((own, one, three))
    )

    near, far, go = add_up(where, grads)
    go = transpose_devices(go)
    gq = (near + swap_lo(far).astype(F32)).astype(BF16)
    mine = jnp.concatenate([gq, go[:ROWS], go[ROWS:]], 1)
    mine = after(mine, two)
    one, three = turn(after(one, mine), 3), turn(after(three, mine), 1)
    every = [mine] + [turn(mine, by) for by in range(1, Z)]
    branch = finish(image, row, (own, one, two, three))
    every += [swap(piece) for piece in every]
    grad_q, grad_o = place([after(mine, branch), *every[1:]], where)
    return branch[None], grad_q, grad_o


def solution(mesh):
    return jax.shard_map(
        body,
        mesh=mesh,
        in_specs=(
            P("dp", "space", None),
            P("dp", "space", None),
            P("dp", None),
            P("dp", None),
            P(),
            P("dp"),
        ),
        out_specs=(P("dp", "space", None), P("dp", None), P("dp", None)),
        check_vma=False,
    )
```

```python
import jax
import jax.numpy as jnp
from jax import lax
from jax.experimental import pallas as pl
from jax.experimental.pallas import tpu as pltpu
from jax.sharding import PartitionSpec as P

C = 1024
Z = 4
XY = 16
ROWS = 32
CELLS = 128
PAIR = 128
QKV = 3 * PAIR
PIECES = 10
F32 = jnp.float32
BF16 = jnp.bfloat16
FAR = pl.BlockSpec(memory_space=pltpu.HBM)
WHOLE = pl.BlockSpec(memory_space=pltpu.VMEM)
SCALARS = pl.BlockSpec(memory_space=pltpu.SMEM)
CHEAP = pl.CostEstimate(flops=0, bytes_accessed=0, transcendentals=0)
SMALL = pltpu.CompilerParams(vmem_limit_bytes=8 * 2**20)
PARAMS = pltpu.CompilerParams(vmem_limit_bytes=58 * 2**20)


def nt(a, b):
    return lax.dot_general(a, b, (((1,), (1,)), ((), ())), preferred_element_type=F32)


def tn(a, b):
    return lax.dot_general(a, b, (((0,), (0,)), ((), ())), preferred_element_type=F32)


def nn(a, b):
    return jnp.dot(a, b, preferred_element_type=F32)


def struct(shape, dtype=BF16):
    return jax.ShapeDtypeStruct(shape, dtype)


def heads():
    lane = lax.broadcasted_iota(jnp.int32, (1, PAIR), 1)
    return lane < PAIR // 2, lane >= PAIR // 2


def project_kernel(where, *refs):
    pieces, parts, (qkvd, wq, wo, x) = refs[:6], refs[6:10], refs[10:]
    for far, part in enumerate(parts):
        col = lax.rem(where[2] - far + 4, 4)
        for lo in range(2):
            half = slice(lo * ROWS, (lo + 1) * ROWS)
            columns = pl.ds(pl.multiple_of((lo * 4 + col) * PAIR, PAIR), PAIR)
            for y in range(4):
                at = pl.multiple_of(((lo * 4 + col) * 4 + y) * ROWS, ROWS)
                wq[pl.ds(at, ROWS), :] = part[y, half, :QKV]
                wo[y * ROWS : (y + 1) * ROWS, columns] = part[y, half, QKV:]
    for i, piece in enumerate(pieces):
        x[i * CELLS : (i + 1) * CELLS, :] = piece[...]
    qkvd[:, :QKV] = nn(x[:, :C], wq[...]).astype(BF16)
    qkvd[:, QKV:] = nt(x[:, C:], wo[...]).astype(BF16)


def project(where, pieces, parts):
    return pl.pallas_call(
        project_kernel,
        in_specs=[SCALARS] + [WHOLE] * 10,
        out_shape=(struct((6 * CELLS, QKV + PAIR)), struct((C, QKV)), struct((PAIR, C))),
        scratch_shapes=[pltpu.VMEM((6 * CELLS, 2 * C), BF16)],
        compiler_params=PARAMS,
        cost_estimate=CHEAP,
    )(where, *pieces, *parts)


def attention_kernel(*refs):
    pieces, rest = refs[:PIECES], refs[PIECES:]
    first, wq_far, wo_far, grads, dqkv_far = rest[:5]
    x, wq, wo, qkv, att, dqkv, turned, sent, sems = rest[5:]
    starts = (0, 128, 256, 320, 384, 512, 640, 768, 832, 896)
    late = (2, 3, 7, 8)
    copies = [pltpu.make_async_copy(wq_far, wq, sems.at[PIECES])]
    copies.append(pltpu.make_async_copy(wo_far, wo, sems.at[PIECES + 1]))
    for i in late:
        to = x.at[starts[i] : starts[i] + pieces[i].shape[0], :]
        copies.append(pltpu.make_async_copy(pieces[i], to, sems.at[i]))
    for i, (at, to, size) in enumerate(
        ((0, 0, 256), (256, 384, 128), (384, 512, 256), (640, 896, 128))
    ):
        source = first.at[at : at + size, :]
        copies.append(
            pltpu.make_async_copy(source, qkv.at[to : to + size, :], sems.at[PIECES + 2 + i])
        )
    rest_of_x = []
    for i in range(PIECES):
        if i not in late:
            to = x.at[starts[i] : starts[i] + pieces[i].shape[0], :]
            rest_of_x.append(pltpu.make_async_copy(pieces[i], to, sems.at[i]))
    for copy in copies + rest_of_x:
        copy.start()
    for copy in copies:
        copy.wait()
    cells = Z * CELLS
    for at in (256, 768):
        rows = slice(at, at + CELLS)
        qkv[rows, :QKV] = nn(x[rows, :C], wq[...]).astype(BF16)
        qkv[rows, QKV:] = nt(x[rows, C:], wo[...]).astype(BF16)
    q = qkv[:, :PAIR] * jnp.bfloat16(0.125)
    k = qkv[:, PAIR : 2 * PAIR]
    v = qkv[:, 2 * PAIR : QKV]
    d = qkv[:, QKV:]
    zero = jnp.zeros_like(q)
    for head, mine_head in enumerate(heads()):
        qh = jnp.where(mine_head, q, zero)
        dh = jnp.where(mine_head, d, zero)
        scores = nt(qh, k)
        e = jnp.exp(scores - jnp.max(scores, -1, keepdims=True))
        p = e * (1.0 / jnp.sum(e, -1, keepdims=True))
        pb = p.astype(BF16)
        o = nn(pb, v).astype(BF16).astype(F32)
        delta = jnp.sum(dh.astype(F32) * o, -1, keepdims=True)
        ds = (p * (nt(dh, v) - delta)).astype(BF16)
        dq = (0.125 * nn(ds, k)).astype(BF16)
        dk, dv = tn(qh, ds), tn(dh, pb)
        if head == 0:
            att[...] = o.astype(BF16)
            dqkv[:, :PAIR] = dq
            turned[:PAIR, :] = dk
            turned[PAIR:, :] = dv
        else:
            att[...] = jnp.where(mine_head, o.astype(BF16), att[...])
            dqkv[:, :PAIR] = jnp.where(mine_head, dq, dqkv[:, :PAIR])
            turned[:PAIR, :] += dk
            turned[PAIR:, :] += dv

    dqkv[:, PAIR:] = turned[...].T.astype(BF16)
    early = pltpu.make_async_copy(dqkv, dqkv_far, sems.at[PIECES])
    early.start()
    for copy in rest_of_x:
        copy.wait()
    grad = tn(dqkv[...], x[:, :C]).T.astype(BF16)
    for lo in range(2):
        for xy in range(XY):
            at = (lo * XY + xy) * ROWS
            sent[xy, lo * ROWS : (lo + 1) * ROWS, :QKV] = grad[at : at + ROWS, :]
    grad = tn(att[...], x[:, C:]).astype(BF16)
    for xy in range(XY):
        col, y = divmod(xy, 4)
        for lo in range(2):
            at = (lo * 4 + col) * PAIR
            sent[xy, lo * ROWS : (lo + 1) * ROWS, QKV:] = grad[
                y * ROWS : (y + 1) * ROWS, at : at + PAIR
            ]
    copy = pltpu.make_async_copy(sent, grads, sems.at[0])
    copy.start()
    copy.wait()
    early.wait()


def terms_kernel(dqkv, wq, far, near, two, own, one, three):
    order = [(Z + 2, far)]
    order += [(Z + spot, near.at[i * CELLS : (i + 1) * CELLS]) for i, spot in enumerate((0, 1, 3))]
    order += [(2, two), (0, own), (1, one), (3, three)]
    for spot, to in order:
        rows = slice(spot * CELLS, (spot + 1) * CELLS)
        to[...] = nt(dqkv[rows, :], wq[...]).astype(BF16)


def dnormed_terms(dqkv, wq):
    return pl.pallas_call(
        terms_kernel,
        out_shape=(
            struct((CELLS, C)),
            struct((3 * CELLS, C)),
            *[struct((CELLS, C))] * Z,
        ),
        compiler_params=pltpu.CompilerParams(vmem_limit_bytes=8 * 2**20),
        cost_estimate=pl.CostEstimate(flops=2**34, bytes_accessed=2**23, transcendentals=0),
    )(dqkv, wq)


def attention(pieces, first, wq, wo):
    cells = 8 * CELLS
    return pl.pallas_call(
        attention_kernel,
        in_specs=[FAR] * (PIECES + 3),
        out_specs=[FAR] * 2,
        out_shape=(struct((XY, 2 * ROWS, QKV + PAIR)), struct((cells, QKV))),
        scratch_shapes=[
            pltpu.VMEM((cells, 2 * C), BF16),
            pltpu.VMEM((C, QKV), BF16),
            pltpu.VMEM((PAIR, C), BF16),
            pltpu.VMEM((cells, QKV + PAIR), BF16),
            pltpu.VMEM((cells, PAIR), BF16),
            pltpu.VMEM((cells, QKV), BF16),
            pltpu.VMEM((2 * PAIR, cells), F32),
            pltpu.VMEM((XY, 2 * ROWS, QKV + PAIR), BF16),
            pltpu.SemaphoreType.DMA((PIECES + 6,)),
        ],
        compiler_params=PARAMS,
        cost_estimate=pl.CostEstimate(
            flops=2**34, bytes_accessed=2**23, transcendentals=2 * cells * cells
        ),
    )(*pieces, first, wq, wo)


def normalize(image, row):
    xf = image.astype(F32)
    centered = xf - jnp.mean(xf, -1, keepdims=True)
    inverse = lax.rsqrt(jnp.mean(centered * centered, -1, keepdims=True) + 1e-05)
    return centered * inverse, inverse, 1.0 + row[:, :C].astype(F32)


def prepare_kernel(image, cot, row, x):
    xhat, _, scale = normalize(image[...], row[...])
    x[:, :C] = (xhat * scale + row[:, C:].astype(F32)).astype(BF16)
    x[:, C:] = cot[...]


def prepare(image, cot, row):
    return pl.pallas_call(
        prepare_kernel,
        in_specs=[WHOLE] * 3,
        out_shape=struct((CELLS, 2 * C)),
        cost_estimate=CHEAP,
        compiler_params=PARAMS,
    )(image, cot, row)


def cut_kernel(w_qkv, w_out, w_part, o_part, sems):
    space = lax.axis_index("space")
    copies = []
    for part in range(3):
        at = pl.multiple_of(part * C + space * PAIR, PAIR)
        to = w_part.at[:, part * PAIR : (part + 1) * PAIR]
        copies.append(pltpu.make_async_copy(w_qkv.at[:, pl.ds(at, PAIR)], to, sems.at[part]))
    for lo in range(2):
        at = pl.multiple_of(lo * 4 * PAIR + lax.rem(space, 4) * PAIR, PAIR)
        to = o_part.at[lo * ROWS : (lo + 1) * ROWS, :]
        copies.append(pltpu.make_async_copy(w_out.at[:, pl.ds(at, PAIR)], to, sems.at[3 + lo]))
    for copy in copies:
        copy.start()
    for copy in copies:
        copy.wait()


def cut(w_qkv, w_out):
    return pl.pallas_call(
        cut_kernel,
        in_specs=[FAR] * 2,
        out_shape=(struct((ROWS, QKV)), struct((2 * ROWS, PAIR))),
        scratch_shapes=[pltpu.SemaphoreType.DMA((5,))],
        cost_estimate=CHEAP,
        compiler_params=PARAMS,
    )(w_qkv, w_out)


def pack_kernel(where, w_part, w_far, o_part, packed):
    low = where[1] == 0
    near, far = w_part[...], w_far[...]
    packed[:ROWS, :QKV] = jnp.where(low, near, far)
    packed[ROWS:, :QKV] = jnp.where(low, far, near)
    packed[:, QKV:] = o_part[...]


def pack(where, w_part, w_far, o_part):
    return pl.pallas_call(
        pack_kernel,
        in_specs=[SCALARS] + [WHOLE] * 3,
        out_shape=struct((2 * ROWS, QKV + PAIR)),
        cost_estimate=CHEAP,
        compiler_params=SMALL,
    )(where, w_part, w_far, o_part)


def join_kernel(where, *refs):
    pieces, joined = refs[:-1], refs[-1]
    for far, piece in enumerate(pieces):
        joined[lax.rem(where[3] - far + 4, 4)] = piece[...]


def join(where, pieces):
    return pl.pallas_call(
        join_kernel,
        in_specs=[SCALARS] + [WHOLE] * 4,
        out_shape=struct((4, 2 * ROWS, QKV + PAIR)),
        cost_estimate=CHEAP,
        compiler_params=SMALL,
    )(where, *pieces)


def total_kernel(where, sent, near, far, go):
    total = sent[0].astype(F32)
    for xy in range(1, XY):
        total = total + sent[xy].astype(F32)
    go[...] = total[:, QKV:].astype(BF16)
    low = where[1] == 0
    first, second = total[:ROWS, :QKV], total[ROWS:, :QKV]
    near[...] = jnp.where(low, first, second)
    far[...] = jnp.where(low, second, first).astype(BF16)


def add_up(where, sent):
    return pl.pallas_call(
        total_kernel,
        in_specs=[SCALARS, WHOLE],
        out_shape=(struct((ROWS, QKV), F32), struct((ROWS, QKV)), struct((2 * ROWS, PAIR))),
        cost_estimate=CHEAP,
        compiler_params=SMALL,
    )(where, sent)


def finish_kernel(image, row, *refs):
    pieces, branch = refs[:-1], refs[-1]
    xhat, inverse, scale = normalize(image[...], row[...])
    dnormed = pieces[0][...].astype(F32)
    for piece in pieces[1:]:
        dnormed = dnormed + piece[...].astype(F32)
    dxhat = dnormed * scale
    mean = jnp.mean(dxhat, -1, keepdims=True)
    along = jnp.mean(dxhat * xhat, -1, keepdims=True)
    branch[...] = (inverse * (dxhat - mean - xhat * along)).astype(BF16)


def finish(image, row, pieces):
    return pl.pallas_call(
        finish_kernel,
        out_shape=struct((CELLS, C)),
        in_specs=[WHOLE] * (2 + len(pieces)),
        cost_estimate=CHEAP,
        compiler_params=SMALL,
    )(image, row, *pieces)


def place_kernel(where, *refs):
    pieces, (grad_q, grad_o) = refs[:-2], refs[-2:]
    z, core = where[0] // 2, lax.rem(where[0], 2)
    lane = lax.broadcasted_iota(jnp.int32, (1, 4 * PAIR), 1) // PAIR
    halves = [jnp.zeros((ROWS, 4 * PAIR), F32), jnp.zeros((ROWS, 4 * PAIR), F32)]
    for i, piece in enumerate(pieces):
        far, other = i % 4, i // 4
        place = lax.rem(z - far + Z, Z) * 2 + (core if other == 0 else 1 - core)
        for part in range(3):
            at = pl.multiple_of(part * C + place * PAIR, PAIR)
            grad_q[:, pl.ds(at, PAIR)] = piece[:, part * PAIR : (part + 1) * PAIR].astype(F32)
        mine = lane == lax.rem(place, 4)
        for lo in range(2):
            at = QKV + lo * PAIR
            value = piece[:, at : at + PAIR].astype(F32)
            halves[lo] = halves[lo] + jnp.where(mine, jnp.concatenate([value] * 4, 1), 0.0)
    grad_o[:, : 4 * PAIR] = halves[0]
    grad_o[:, 4 * PAIR :] = halves[1]


def place(pieces, where):
    return pl.pallas_call(
        place_kernel,
        in_specs=[SCALARS] + [WHOLE] * 8,
        out_shape=(struct((ROWS, 3 * C), F32), struct((ROWS, C), F32)),
        cost_estimate=CHEAP,
        compiler_params=SMALL,
    )(where, *pieces)


def turn(x, by):
    pairs = [(z * 2 + c, (z + by) % Z * 2 + c) for z in range(Z) for c in range(2)]
    return lax.ppermute(x, "space", pairs)


def swap(x):
    return lax.ppermute(x, "space", [(i, i ^ 1) for i in range(2 * Z)])


def swap_lo(x):
    return lax.ppermute(x, "dp", [(i, i ^ XY) for i in range(2 * XY)])


def transpose_devices(x):
    at = lambda t, y, s: (t * 4 + y) * 8 + s
    pairs = [(at(t, y, s), at(s, y, t)) for t in range(8) for y in range(4) for s in range(8)]
    return lax.ppermute(x, ("dp", "space"), pairs)


def turn_dp(x, by_x, by_y):
    at = lambda lo, col, y: (lo * 4 + col % 4) * 4 + y % 4
    pairs = [
        (at(lo, col, y), at(lo, col + by_x, y + by_y))
        for lo in range(2)
        for col in range(4)
        for y in range(4)
    ]
    return lax.ppermute(x, "dp", pairs)


def over_xy(x):
    groups = [list(range(XY)), list(range(XY, 2 * XY))]
    return lax.all_to_all(x, "dp", 0, 0, axis_index_groups=groups, tiled=True)


def add(a, b):
    return (a.astype(F32) + b.astype(F32)).astype(BF16)


def after(x, *others):
    return lax.optimization_barrier((x, others))[0]


def body(images, cotangent, w_qkv, w_out, film, timesteps):
    space, dp = lax.axis_index("space"), lax.axis_index("dp")
    where = jnp.stack([space, dp // XY, lax.rem(dp // 4, 4), lax.rem(dp, 4)])
    row = lax.dynamic_slice_in_dim(film, timesteps[0], 1, 0)
    image = images[0]
    w_part, o_part = cut(w_qkv, w_out)
    w_far, o_part = swap_lo(w_part), transpose_devices(o_part)
    x = prepare(image, cotangent[0], row)
    x = after(x, w_far, o_part)
    one, three = turn(x, 1), turn(x, 3)
    packed = pack(where, w_part, w_far, o_part)
    packed = [packed] + [turn_dp(packed, 0, by) for by in range(1, 4)]
    parts = join(where, packed)
    x = after(x, *packed)
    parts = [parts] + [turn_dp(parts, by, 0) for by in range(1, 4)]
    one, three = after((one, three), *parts)
    half = CELLS // 2
    two = turn(one[:half], 1), turn(three[half:], 3)
    others = [swap(piece) for piece in (x, one, three)]
    first, wq, wo = project(where, [x, one, three, *others], parts)
    two = after(two, first)
    pieces = [x, one, *two, three]
    pieces += [others[0], others[1], *[swap(piece) for piece in two], others[2]]
    grads, dqkv = attention(pieces, first, wq, wo)
    grads = over_xy(grads)
    far, near, two, own, one, three = dnormed_terms(dqkv, wq)

    two = turn(add(two, swap(far)), 2)
    near = swap(near)
    own, one, three = (
        add(piece, near[i * CELLS : (i + 1) * CELLS]) for i, piece in enumerate((own, one, three))
    )

    near, far, go = add_up(where, grads)
    go = transpose_devices(go)
    gq = (near + swap_lo(far).astype(F32)).astype(BF16)
    mine = jnp.concatenate([gq, go[:ROWS], go[ROWS:]], 1)
    mine = after(mine, two)
    one, three = turn(after(one, mine), 3), turn(after(three, mine), 1)
    every = [mine] + [turn(mine, by) for by in range(1, Z)]
    branch = finish(image, row, (own, one, two, three))
    every += [swap(piece) for piece in every]
    grad_q, grad_o = place([after(mine, branch), *every[1:]], where)
    return branch[None], grad_q, grad_o


def solution(mesh):
    return jax.shard_map(
        body,
        mesh=mesh,
        in_specs=(
            P("dp", "space", None),
            P("dp", "space", None),
            P("dp", None),
            P("dp", None),
            P(),
            P("dp"),
        ),
        out_specs=(P("dp", "space", None), P("dp", None), P("dp", None)),
        check_vma=False,
    )
```
